512 devices in a mesh: grp: 16 (over x, y_hi), tile: 32 (over z, y_lo, core).
Axes of the slice: x: 4, y: 8 (y_hi: 4, y_lo: 2; y = y_hi * 2 + y_lo), z: 8, core: 2. Of those that a mesh axis runs over, the one named last changes fastest.
Arguments:
- base_velocity: float32 [2, 1024, 4096], P(None, 'grp', 'tile'), may hold values from -6 to 6
- viscosity: float32 [1024, 4096], P('grp', 'tile'), may hold values from 0.5 to 2
- friction: float32 [1024, 4096], P('grp', 'tile'), may hold values from 2 to 8
- friction_probe: float32 [1024, 4096], P('grp', 'tile'), may hold values from -6 to 6
- pixel_los: float32 [16, 32, 2, 2048], P('grp', 'tile'), may hold values from -6 to 6
- pixel_weight: float32 [16, 32, 1, 2048], P('grp', 'tile'), may hold values from 2 to 20
- pixel_cell: int32 [16, 32, 1, 2048], P('grp', 'tile'), may hold values from 0 to 8191
- pixel_count: int32 [16, 32, 1, 32], P('grp', 'tile'), may hold values from 8 to 64, as said below
- panels: bfloat16 [128, 1024, 4096], P('grp', None, 'tile'), may hold values from -0.00390625 to 0.00390625
Outputs:
- increment: float32 [2, 1024, 4096], P(None, 'grp', 'tile')
- hessian_probe: float32 [1024, 4096], P('grp', 'tile')
- coefficients: float32 [128], replicated
The draws below stay inside these ranges and needn't reach their ends.
Inputs may be any that keep to these rules, and one draw needn't show every extreme that they name: In group g, tile s uses the first pixel_count[g, s, 0, o] of its 64 slots toward owner tile o; in every group some owner receives 64 from every tile, and such owners are a few times busier than the mean. `pixel_cell`: cells are numbered row by row within the owner's block of 64 x 128 cells.
All inputs are finite; a program needn't handle non-finite values.
Results may differ from the reference program's by a relative error of at most 0.0036.
Values may be sent and summed in bfloat16 or wider, within the bound.
A program may use at most 64 MiB of HBM per device.

```python
import math
import jax
import jax.numpy as jnp

CX = 64
CY = 128
CAP = 64
K = 128
SWEEPS = 8
NX = 1024
NY = 4096
SLOTS = 2048
N_GRP = 16
N_TILE = 32


def draw_pixel_count(key, part):
    key = jax.random.fold_in(key, 7)
    key_base, key_hot, key_forced = jax.random.split(key, 3)
    base = jax.random.randint(key_base, (N_GRP, N_TILE, 1, N_TILE), CAP // 8, CAP // 2 + 1)
    busy = jax.random.randint(key_hot, (N_GRP, 1, 1, N_TILE), 0, 8) == 0
    forced = jax.random.randint(key_forced, (N_GRP, 1, 1, 1), 0, N_TILE)
    busy = busy | (jnp.arange(N_TILE)[None, None, None, :] == forced)
    return jnp.where(busy, CAP, base).astype(jnp.int32)


def plant(entries, own_key, smallest, top_value):
    longest = entries.shape.index(max(entries.shape))
    spots = []
    for shift in (0, 1):
        where = [jax.random.randint(jax.random.fold_in(own_key, axis), (), 0, length) for axis, length in enumerate(entries.shape)]
        where[longest] = (where[longest] + shift) % entries.shape[longest]
        spots.append(tuple(where))
    return entries.at[spots[0]].set(smallest).at[spots[1]].set(top_value)


def strengthened(entries, stream_key, source, target, blocks, factor):
    def block_of(position):
        return (jnp.arange(entries.shape[position]) // (entries.shape[position] // blocks)).reshape((-1,) + (1,) * (entries.ndim - 1 - position))

    near = jax.random.permutation(stream_key, blocks)[block_of(target)]
    far = (block_of(target) + blocks // 2) % blocks
    return jnp.where((block_of(source) == near) | (block_of(source) == far), factor * entries, entries)


def level_of(key, extent, cuts, low, high):
    gain = 1.0
    for dim, blocks in cuts:
        draws = jax.random.uniform(jax.random.fold_in(jax.random.fold_in(key, 6), dim), (blocks,), jnp.float32, low / len(cuts), high / len(cuts))
        gain = gain * jnp.repeat(jnp.exp(draws), extent[dim] // blocks).reshape((-1,) + (1,) * (len(extent) - 1 - dim))
    return gain


def gaussian(rng, shape, width, limit, cuts=(), kind=jnp.bfloat16):
    result = width * jax.random.normal(rng, shape, jnp.float32)
    if cuts:
        result = result * level_of(rng, shape, cuts, -0.22, 0.18)
    return jnp.clip(result, -limit, limit).astype(kind)


def bell_draw_with(stream_key, shape, width, most, pieces, heavy, kind=jnp.bfloat16):
    values = width * jax.random.normal(stream_key, shape, jnp.float32)
    if pieces:
        values = values * level_of(stream_key, shape, pieces, -0.22, 0.18)
    return jnp.clip(strengthened(values, jax.random.fold_in(stream_key, 3), *heavy), -most, most).astype(kind)


def setup_inputs(seed: int = 0) -> dict:
    splits = jax.random.split(jax.random.key(seed), 10)
    return {
        "base_velocity": gaussian(splits[0], (2, NX, NY), 1.0, 6.0, ((1, 16), (2, 32)), jnp.float32),
        "viscosity": jnp.clip(jnp.exp(math.log(2.0) - 1.3862944 * jax.random.uniform(splits[1], (NX, NY), jnp.float32) ** level_of(splits[1], (NX, NY), ((0, 16), (1, 32)), -0.2, 0.2)), 0.5, 2.0),
        "friction": jnp.clip(jnp.exp(math.log(8.0) - 1.3862944 * jax.random.uniform(splits[2], (NX, NY), jnp.float32) ** level_of(splits[2], (NX, NY), ((0, 16), (1, 32)), -0.2, 0.2)), 2.0, 8.0),
        "friction_probe": gaussian(splits[3], (NX, NY), 1.0, 6.0, ((0, 16), (1, 32)), jnp.float32),
        "pixel_los": gaussian(splits[4], (N_GRP, N_TILE, 2, SLOTS), 1.0, 6.0, ((0, 16), (1, 32)), jnp.float32),
        "pixel_weight": jnp.clip(jnp.exp(math.log(20.0) - 2.3025851 * jax.random.uniform(splits[5], (N_GRP, N_TILE, 1, SLOTS), jnp.float32) ** level_of(splits[5], (N_GRP, N_TILE, 1, SLOTS), ((0, 16), (1, 32)), -0.2, 0.2)), 2.0, 20.0),
        "pixel_cell": plant(jax.random.randint(splits[6], (N_GRP, N_TILE, 1, SLOTS), 0, CX * CY), jax.random.fold_in(splits[6], 1), 0, (CX * CY) - 1).astype(jnp.int32),
        "pixel_count": draw_pixel_count(jax.random.fold_in(splits[9], 71), 0),
        "panels": bell_draw_with(splits[8], (K, NX, NY), (NX * NY) ** -0.5, 0.00390625, ((0, 16), (2, 32)), (1, 0, 16, 2.0)),
    }


relax_weight = 0.8


def face_terms(visc_ext, fric_inner):
    centre = visc_ext[1:-1, 1:-1]
    east = 0.5 * (centre + visc_ext[2:, 1:-1])
    west = 0.5 * (centre + visc_ext[:-2, 1:-1])
    north = 0.5 * (centre + visc_ext[1:-1, 2:])
    south = 0.5 * (centre + visc_ext[1:-1, :-2])
    node_pp = 0.25 * (centre + visc_ext[2:, 1:-1] + visc_ext[1:-1, 2:] + visc_ext[2:, 2:])
    node_mm = 0.25 * (centre + visc_ext[:-2, 1:-1] + visc_ext[1:-1, :-2] + visc_ext[:-2, :-2])
    node_pm = 0.25 * (centre + visc_ext[2:, 1:-1] + visc_ext[1:-1, :-2] + visc_ext[2:, :-2])
    node_mp = 0.25 * (centre + visc_ext[:-2, 1:-1] + visc_ext[1:-1, 2:] + visc_ext[:-2, 2:])
    diag_x = fric_inner + 2.0 * (east + west) + (north + south)
    diag_y = fric_inner + (east + west) + 2.0 * (north + south)
    return jnp.stack([east, west, north, south, node_pp, node_mm, node_pm, node_mp, diag_x, diag_y])


def operate(field_ext, terms):
    east, west, north, south = terms[0], terms[1], terms[2], terms[3]
    node_pp, node_mm, node_pm, node_mp = terms[4], terms[5], terms[6], terms[7]
    first = field_ext[0]
    second = field_ext[1]

    def axial(comp, along_one, along_two):
        return along_one * (east * comp[2:, 1:-1] + west * comp[:-2, 1:-1]) + along_two * (north * comp[1:-1, 2:] + south * comp[1:-1, :-2])

    def cross(comp):
        return node_pp * comp[2:, 2:] + node_mm * comp[:-2, :-2] - node_pm * comp[2:, :-2] - node_mp * comp[:-2, 2:]

    out_first = terms[8] * first[1:-1, 1:-1] - axial(first, 2.0, 1.0) - 0.25 * cross(second)
    out_second = terms[9] * second[1:-1, 1:-1] - axial(second, 1.0, 2.0) - 0.25 * cross(first)
    return jnp.stack([out_first, out_second])


def relax(source, terms):
    field = jnp.zeros(source.shape, jnp.float32)
    diagonal = terms[8:10]
    for sweep in range(SWEEPS):
        padded = jnp.pad(field, ((0, 0), (1, 1), (1, 1)))
        field = field + relax_weight * (source - operate(padded, terms)) / diagonal
    return field


def reference(base_velocity, viscosity, friction, friction_probe, pixel_los, pixel_weight, pixel_cell, pixel_count, panels):
    terms = face_terms(jnp.pad(viscosity, 1), friction)
    source = -(friction_probe[None] * base_velocity)
    increment = relax(source, terms)
    los = pixel_los.reshape(N_GRP, N_TILE, 2, N_TILE, CAP)
    weight = pixel_weight.reshape(N_GRP, N_TILE, N_TILE, CAP)
    cell = pixel_cell.reshape(N_GRP, N_TILE, N_TILE, CAP)
    count = pixel_count.reshape(N_GRP, N_TILE, N_TILE)
    live = jnp.arange(CAP, dtype=jnp.int32)[None, None, None, :] < count[..., None]
    group = jnp.arange(N_GRP, dtype=jnp.int32)[:, None, None, None]
    owner = jnp.arange(N_TILE, dtype=jnp.int32)[None, None, :, None]
    row_ids = group * CX + cell // CY
    col_ids = owner * CY + cell % CY
    spot = (row_ids * NY + col_ids).reshape(-1).astype(jnp.int32)
    flat = increment.reshape(2, -1)
    los_x = los[:, :, 0].reshape(-1)
    los_y = los[:, :, 1].reshape(-1)
    predicted = los_x * flat[0][spot] + los_y * flat[1][spot]
    amount = jnp.where(live.reshape(-1), weight.reshape(-1) * predicted, 0.0)
    adjoint_source = jnp.zeros((2, NX * NY), jnp.float32).at[:, spot].add(jnp.stack([amount * los_x, amount * los_y])).reshape(2, NX, NY)
    multiplier = relax(adjoint_source, terms)
    hessian_probe = -(base_velocity[0] * multiplier[0] + base_velocity[1] * multiplier[1])
    probe_low = hessian_probe.astype(jnp.bfloat16)
    coefficients = jnp.dot(panels.reshape(K, -1), probe_low.reshape(-1), preferred_element_type=jnp.float32)
    return increment, hessian_probe, coefficients
```

```python
import functools

import jax
import jax.numpy as jnp
from jax import lax
from jax.experimental import pallas as pl
from jax.experimental.pallas import tpu as pltpu
from jax.sharding import PartitionSpec as P

SWEEPS = 8
RELAX = 0.8
HALO = 8
CAP = 64
LANES = 128
MESH = pl.DeviceIdType.MESH
F32 = jnp.float32
BF16 = jnp.bfloat16


def lane_of(shape):
    return lax.broadcasted_iota(jnp.int32, shape, 1)


def row_of(shape):
    return lax.broadcasted_iota(jnp.int32, shape, 0)


def row_next(a):
    return pltpu.roll(a, a.shape[0] - 1, 0)


def row_prev(a):
    return pltpu.roll(a, 1, 0)


def col_next(a):
    return pltpu.roll(a, a.shape[1] - 1, 1)


def col_prev(a):
    return pltpu.roll(a, 1, 1)


def pack_rims(fields):
    lane = lane_of(fields[0].shape)
    packed = fields[0]
    for index, field in enumerate(fields[1:], 1):
        moved = pltpu.roll(field, 16 * index, 1)
        here = (lane >= 16 * index - 8) & (lane < 16 * index + 8)
        packed = jnp.where(here, moved, packed)
    return packed


def kernel(
    n_grp,
    n_tile,
    base_velocity,
    viscosity,
    friction,
    friction_probe,
    pixel_los,
    pixel_weight,
    pixel_cell,
    pixel_count,
    panels,
    increment_out,
    probe_out,
    coef_out,
    ext,
    pack,
    side_r,
    side_l,
    slots_out,
    slots_in,
    coef,
    src,
    field,
    inc_stage,
    ext2,
    pack2,
    side2_r,
    side2_l,
    probe_stage,
    low_stage,
    column,
    panel_buf,
    part_stage,
    part_in,
    sum_stage,
    sum_in,
    halo_send,
    halo_recv,
    halo2_send,
    halo2_recv,
    local_sem,
    many_send,
    many_recv,
):
    g = lax.axis_index("grp")
    t = lax.axis_index("tile")
    up = lax.rem(g + n_grp - 1, n_grp)
    down = lax.rem(g + 1, n_grp)
    left = lax.rem(t + n_tile - 1, n_tile)
    right = lax.rem(t + 1, n_tile)

    barrier = pltpu.get_barrier_semaphore()

    def greet_tile(k, carry):
        pl.semaphore_signal(barrier, inc=1, device_id=(g, lax.rem(t + k, n_tile)), device_id_type=MESH)
        return carry

    def greet_grp(k, carry):
        pl.semaphore_signal(barrier, inc=1, device_id=(lax.rem(g + k, n_grp), t), device_id_type=MESH)
        return carry

    for a in (up, down):
        for b in (left, right):
            pl.semaphore_signal(barrier, inc=1, device_id=(a, b), device_id_type=MESH)
    lax.fori_loop(1, n_grp, greet_grp, 0)
    lax.fori_loop(1, n_tile, greet_tile, 0)

    panel_copy = pltpu.make_async_copy(panels, panel_buf, local_sem.at[0])
    panel_copy.start()

    bvx = base_velocity[0]
    bvy = base_velocity[1]
    fp = friction_probe[...]
    own = (viscosity[...], friction[...], -(fp * bvx), -(fp * bvy))
    for index in range(4):
        ext[index, HALO : HALO + 64, :] = own[index]
    pack[...] = pack_rims(own)

    odd = lax.rem(t, 2)
    lane1 = lane_of((1, LANES))
    for pair in range(n_tile // 2):
        lanes = slice(pair * LANES, (pair + 1) * LANES)
        count = jnp.where(lane1 < CAP, pixel_count[0, 2 * pair], pixel_count[0, 2 * pair + 1])
        live = lax.rem(lane1, CAP) < count
        block = jnp.concatenate(
            [
                pixel_los[:, lanes],
                jnp.where(live, pixel_weight[:, lanes], 0.0),
                pixel_cell[:, lanes].astype(F32),
            ],
            axis=0,
        )
        slots_out[pair] = jnp.where(odd == 1, pltpu.roll(block, CAP, 1), block)

    pl.semaphore_wait(barrier, n_tile - 1 + n_grp - 1 + 4)

    def rim_copies(block, packed, from_right, from_left, send, recv):
        first, last = pl.ds(HALO, HALO), pl.ds(64, HALO)
        above, middle, below = pl.ds(0, HALO), pl.ds(HALO, 64), pl.ds(64 + HALO, HALO)
        head, tail = pl.ds(0, HALO), pl.ds(64 - HALO, HALO)
        moves = [
            (block.at[:, first], block.at[:, below], (up, t)),
            (block.at[:, last], block.at[:, above], (down, t)),
            (packed, from_right.at[middle], (g, left)),
            (packed, from_left.at[middle], (g, right)),
            (packed.at[head], from_right.at[below], (up, left)),
            (packed.at[head], from_left.at[below], (up, right)),
            (packed.at[tail], from_right.at[above], (down, left)),
            (packed.at[tail], from_left.at[above], (down, right)),
        ]
        return [
            pltpu.make_async_remote_copy(
                src_ref=a,
                dst_ref=b,
                send_sem=send.at[index],
                recv_sem=recv.at[index],
                device_id=target,
                device_id_type=MESH,
            )
            for index, (a, b, target) in enumerate(moves)
        ]

    def wait_bytes(ref, sem):
        pltpu.make_async_copy(ref, ref, sem).wait()

    copies = rim_copies(ext, pack, side_r, side_l, halo_send, halo_recv)
    for copy in copies:
        copy.start()

    def send_list(k, carry):
        owner = lax.rem(t + k, n_tile)
        pltpu.make_async_remote_copy(
            src_ref=slots_out.at[lax.div(owner, 2)],
            dst_ref=slots_in.at[k],
            send_sem=many_send.at[0],
            recv_sem=many_recv.at[0],
            device_id=(g, owner),
            device_id_type=MESH,
        ).start()
        return carry

    lax.fori_loop(1, n_tile, send_list, 0)
    slots_in[0] = slots_out[lax.div(t, 2)]

    for copy in copies:
        copy.wait_recv()

    rows = 64 + 2 * HALO
    lane = lane_of((rows, LANES))
    row = row_of((rows, LANES))

    def widen(block, from_right, from_left):
        merged = jnp.where(lax.rem(lane, 16) < 8, from_right[...], from_left[...])
        fields = []
        for index in range(block.shape[0]):
            beside = merged if index == 0 else pltpu.roll(merged, LANES - 16 * index, 1)
            fields.append(jnp.concatenate([block[index], beside], axis=1))
        return fields

    v, fr, sx, sy = widen(ext, side_r, side_l)
    row_inside = ((row >= HALO) | (g > 0)) & ((row < HALO + 64) | (g < n_grp - 1))
    col_inside = ((lane < HALO) & (t < n_tile - 1)) | ((lane >= LANES - HALO) & (t > 0))
    inside = jnp.concatenate([row_inside, row_inside & col_inside], axis=1)
    v = jnp.where(inside, v, 0.0)
    pair_sum = v + row_next(v)
    east = 0.5 * pair_sum
    west = row_prev(east)
    north = 0.5 * (v + col_next(v))
    south = col_prev(north)
    node_pp = 0.0625 * (pair_sum + col_next(pair_sum))
    node_mp = row_prev(node_pp)
    node_pm = col_prev(node_pp)
    node_mm = col_prev(node_mp)
    diag_x = fr + 2.0 * (east + west) + (north + south)
    diag_y = fr + (east + west) + 2.0 * (north + south)
    inv_x = jnp.where(inside, RELAX / jnp.where(inside, diag_x, 1.0), 0.0)
    inv_y = jnp.where(inside, RELAX / jnp.where(inside, diag_y, 1.0), 0.0)
    for index, term in enumerate((east, west, north, south, node_pp, node_mp, node_pm, node_mm, inv_x, inv_y)):
        coef[index] = term
    src[0] = sx
    src[1] = sy

    def sweep(_, carry):
        cx, cy = field[0], field[1]
        ux, uy = row_next(cx), row_next(cy)
        dx, dy = row_prev(cx), row_prev(cy)
        e, w, n, s = coef[0], coef[1], coef[2], coef[3]
        pp, mp, pm, mm = coef[4], coef[5], coef[6], coef[7]
        ax = 2.0 * (e * ux + w * dx)
        ax += col_next(s * cx + (pm * uy - mm * dy))
        ax += col_prev(n * cx + (mp * dy - pp * uy))
        ay = e * uy + w * dy
        ay += col_next(2.0 * (s * cy) + (pm * ux - mm * dx))
        ay += col_prev(2.0 * (n * cy) + (mp * dx - pp * ux))
        field[0] = (1.0 - RELAX) * cx + coef[8] * (src[0] + ax)
        field[1] = (1.0 - RELAX) * cy + coef[9] * (src[1] + ay)
        return carry

    def relax():
        field[0] = coef[8] * src[0]
        field[1] = coef[9] * src[1]
        lax.fori_loop(1, SWEEPS, sweep, 0)
        return field[0, HALO : HALO + 64, :LANES], field[1, HALO : HALO + 64, :LANES]

    inc_x, inc_y = relax()
    inc_stage[0] = inc_x
    inc_stage[1] = inc_y
    increment_copy = pltpu.make_async_copy(inc_stage, increment_out, local_sem.at[1])
    increment_copy.start()

    wait_bytes(slots_in.at[pl.ds(0, n_tile - 1)], many_recv.at[0])

    def halves(a):
        high = a.astype(BF16)
        return high, (a - high.astype(F32)).astype(BF16)

    xh, xl = halves(inc_x)
    yh, yl = halves(inc_y)
    stacked = jnp.concatenate([xh, yh, xl, yl], axis=0)
    chunk = 2 * LANES
    total = jnp.zeros((256, LANES), F32)
    low_half = lane_of((4, LANES)) < CAP
    for index in range(n_tile * CAP // chunk):
        first = jnp.where(low_half, slots_in[4 * index], slots_in[4 * index + 1])
        second = jnp.where(low_half, slots_in[4 * index + 2], slots_in[4 * index + 3])
        lists = jnp.concatenate([first, second], axis=1)
        los_x, los_y, weight = lists[0:1], lists[1:2], lists[2:3]
        cell = lists[3:4].astype(jnp.int32)
        at_col = row_of((LANES, chunk)) == (cell & (LANES - 1))
        at_row = row_of((64, chunk)) == (cell >> 7)
        col_hot = jnp.where(at_col, 1.0, 0.0).astype(BF16)
        found = jnp.dot(stacked, col_hot, preferred_element_type=F32)
        got_x = jnp.sum(jnp.where(at_row, found[0:64] + found[128:192], 0.0), axis=0, keepdims=True)
        got_y = jnp.sum(jnp.where(at_row, found[64:128] + found[192:256], 0.0), axis=0, keepdims=True)
        amount = weight * (los_x * got_x + los_y * got_y)
        scaled = []
        for value in (amount * los_x, amount * los_y):
            high = value.astype(BF16).astype(F32)
            scaled.append((high, value - high))
        hot = [
            jnp.where(at_row, jnp.broadcast_to(part, (64, chunk)), 0.0)
            for part in (scaled[0][0], scaled[1][0], scaled[0][1], scaled[1][1])
        ]
        hot = jnp.concatenate(hot, axis=0).astype(BF16)
        total += lax.dot_general(hot, col_hot, (((1,), (1,)), ((), ())), preferred_element_type=F32)
    adjoint = (total[0:64] + total[128:192], total[64:128] + total[192:256])

    for index in range(2):
        ext2[index, HALO : HALO + 64, :] = adjoint[index]
    pack2[...] = pack_rims(adjoint)
    copies2 = rim_copies(ext2, pack2, side2_r, side2_l, halo2_send, halo2_recv)
    for copy in copies2:
        copy.start()
    for copy in copies2:
        copy.wait_recv()
    sx2, sy2 = widen(ext2, side2_r, side2_l)
    src[0] = sx2
    src[1] = sy2
    mult_x, mult_y = relax()

    probe = -(base_velocity[0] * mult_x + base_velocity[1] * mult_y)
    probe_low = probe.astype(BF16)
    low_stage[...] = probe_low
    column[g] = probe_low

    def send_probe(k, carry):
        peer = lax.rem(g + k, n_grp)
        pltpu.make_async_remote_copy(
            src_ref=low_stage,
            dst_ref=column.at[g],
            send_sem=many_send.at[1],
            recv_sem=many_recv.at[1],
            device_id=(peer, t),
            device_id_type=MESH,
        ).start()
        return carry

    lax.fori_loop(1, n_grp, send_probe, 0)
    probe_stage[...] = probe
    probe_copy = pltpu.make_async_copy(probe_stage, probe_out, local_sem.at[2])
    probe_copy.start()
    panel_copy.wait()
    wait_bytes(column.at[pl.ds(0, n_grp - 1)], many_recv.at[1])

    def project(block, sums):
        values = column[block].astype(F32)
        start = pl.multiple_of(block * 64, 64)
        return tuple(
            total + jnp.sum((panel_buf[k, pl.ds(start, 64), :].astype(F32) * values).reshape(8, 8, LANES), axis=0)
            for k, total in enumerate(sums)
        )

    sums = lax.fori_loop(0, n_grp, project, tuple(jnp.zeros((8, LANES), F32) for _ in range(8)))
    partial = jnp.concatenate([jnp.sum(s, axis=0, keepdims=True) for s in sums], axis=0)
    part_stage[...] = partial
    part_in[t] = partial

    def send_part(k, carry):
        peer = lax.rem(t + k, n_tile)
        pltpu.make_async_remote_copy(
            src_ref=part_stage,
            dst_ref=part_in.at[t],
            send_sem=many_send.at[2],
            recv_sem=many_recv.at[2],
            device_id=(g, peer),
            device_id_type=MESH,
        ).start()
        return carry

    lax.fori_loop(1, n_tile, send_part, 0)
    wait_bytes(part_in.at[pl.ds(0, n_tile - 1)], many_recv.at[2])
    summed = jnp.sum(jnp.sum(part_in[...], axis=0), axis=1, keepdims=True)
    mine = lane_of((8, LANES)) == 8 * g + row_of((8, LANES))
    placed = jnp.where(mine, jnp.broadcast_to(summed, (8, LANES)), 0.0)
    sum_stage[...] = placed
    sum_in[g] = placed

    def send_sum(k, carry):
        peer = lax.rem(g + k, n_grp)
        pltpu.make_async_remote_copy(
            src_ref=sum_stage,
            dst_ref=sum_in.at[g],
            send_sem=many_send.at[3],
            recv_sem=many_recv.at[3],
            device_id=(peer, t),
            device_id_type=MESH,
        ).start()
        return carry

    lax.fori_loop(1, n_grp, send_sum, 0)
    wait_bytes(sum_in.at[pl.ds(0, n_grp - 1)], many_recv.at[3])
    coef_out[...] = jnp.sum(jnp.sum(sum_in[...], axis=0), axis=0, keepdims=True)

    for copy in copies + copies2:
        copy.wait_send()
    wait_bytes(slots_in.at[pl.ds(0, n_tile - 1)], many_send.at[0])
    wait_bytes(column.at[pl.ds(0, n_grp - 1)], many_send.at[1])
    wait_bytes(part_in.at[pl.ds(0, n_tile - 1)], many_send.at[2])
    wait_bytes(sum_in.at[pl.ds(0, n_grp - 1)], many_send.at[3])
    increment_copy.wait()
    probe_copy.wait()


def on_device(n_grp, n_tile, base_velocity, viscosity, friction, friction_probe, pixel_los, pixel_weight, pixel_cell, pixel_count, panels):
    slots = pixel_los.shape[-1]
    panel_rows = panels.shape[1]
    vmem = pl.BlockSpec(memory_space=pltpu.VMEM)
    anywhere = pl.BlockSpec(memory_space=pl.ANY)
    wide = 64 + 2 * HALO
    increment, probe, coefficients = pl.pallas_call(
        functools.partial(kernel, n_grp, n_tile),
        out_shape=(
            jax.ShapeDtypeStruct((2, 64, LANES), F32),
            jax.ShapeDtypeStruct((64, LANES), F32),
            jax.ShapeDtypeStruct((1, LANES), F32),
        ),
        in_specs=[vmem] * 7 + [pl.BlockSpec(memory_space=pltpu.SMEM), anywhere],
        out_specs=(anywhere, anywhere, vmem),
        scratch_shapes=[
            pltpu.VMEM((4, wide, LANES), F32),
            pltpu.VMEM((64, LANES), F32),
            pltpu.VMEM((wide, LANES), F32),
            pltpu.VMEM((wide, LANES), F32),
            pltpu.VMEM((n_tile // 2, 4, LANES), F32),
            pltpu.VMEM((n_tile, 4, LANES), F32),
            pltpu.VMEM((10, wide, 2 * LANES), F32),
            pltpu.VMEM((2, wide, 2 * LANES), F32),
            pltpu.VMEM((2, wide, 2 * LANES), F32),
            pltpu.VMEM((2, 64, LANES), F32),
            pltpu.VMEM((2, wide, LANES), F32),
            pltpu.VMEM((64, LANES), F32),
            pltpu.VMEM((wide, LANES), F32),
            pltpu.VMEM((wide, LANES), F32),
            pltpu.VMEM((64, LANES), F32),
            pltpu.VMEM((64, LANES), BF16),
            pltpu.VMEM((n_grp, 64, LANES), BF16),
            pltpu.VMEM((8, panel_rows, LANES), BF16),
            pltpu.VMEM((8, LANES), F32),
            pltpu.VMEM((n_tile, 8, LANES), F32),
            pltpu.VMEM((8, LANES), F32),
            pltpu.VMEM((n_grp, 8, LANES), F32),
            pltpu.SemaphoreType.DMA((8,)),
            pltpu.SemaphoreType.DMA((8,)),
            pltpu.SemaphoreType.DMA((8,)),
            pltpu.SemaphoreType.DMA((8,)),
            pltpu.SemaphoreType.DMA((3,)),
            pltpu.SemaphoreType.DMA((4,)),
            pltpu.SemaphoreType.DMA((4,)),
        ],
        compiler_params=pltpu.CompilerParams(
            collective_id=0, has_side_effects=True, vmem_limit_bytes=24 * 1024 * 1024
        ),
    )(
        base_velocity,
        viscosity,
        friction,
        friction_probe,
        pixel_los.reshape(2, slots),
        pixel_weight.reshape(1, slots),
        pixel_cell.reshape(1, slots),
        pixel_count.reshape(1, n_tile),
        panels,
    )
    return increment, probe, coefficients.reshape(LANES)[: 8 * n_grp]


def solution(mesh):
    in_specs = (
        P(None, "grp", "tile"),
        P("grp", "tile"),
        P("grp", "tile"),
        P("grp", "tile"),
        P("grp", "tile", None, None),
        P("grp", "tile", None, None),
        P("grp", "tile", None, None),
        P("grp", "tile", None, None),
        P("grp", None, "tile"),
    )
    out_specs = (P(None, "grp", "tile"), P("grp", "tile"), P())
    body = functools.partial(on_device, mesh.shape["grp"], mesh.shape["tile"])
    return jax.shard_map(body, mesh=mesh, in_specs=in_specs, out_specs=out_specs, check_vma=False)
```

```python
import functools

import jax
import jax.numpy as jnp
from jax import lax
from jax.experimental import pallas as pl
from jax.experimental.pallas import tpu as pltpu
from jax.sharding import PartitionSpec as P

SWEEPS = 8
RELAX = 0.8
HALO = 8
CAP = 64
LANES = 128
MESH = pl.DeviceIdType.MESH
F32 = jnp.float32
BF16 = jnp.bfloat16


def lane_of(shape):
    return lax.broadcasted_iota(jnp.int32, shape, 1)


def row_of(shape):
    return lax.broadcasted_iota(jnp.int32, shape, 0)


def row_next(a):
    return pltpu.roll(a, a.shape[0] - 1, 0)


def row_prev(a):
    return pltpu.roll(a, 1, 0)


def col_next(a):
    return pltpu.roll(a, a.shape[1] - 1, 1)


def col_prev(a):
    return pltpu.roll(a, 1, 1)


def pack_rims(fields):
    lane = lane_of(fields[0].shape)
    packed = pltpu.roll(fields[0], 8, 1)
    for index, field in enumerate(fields[1:], 1):
        moved = pltpu.roll(field, 16 * index + 8, 1)
        packed = jnp.where(lane >= 16 * index, moved, packed)
    return packed


def fold_rows(packed, width):
    high = width // 2
    folded = packed[0:high]
    lane = lane_of(folded.shape)
    for index in range(1, LANES // width):
        moved = pltpu.roll(packed[index * high : (index + 1) * high], index * width, 1)
        folded = jnp.where(lane >= index * width, moved, folded)
    return folded


def unfold_rows(folded, width):
    parts = [folded] + [pltpu.roll(folded, LANES - index * width, 1) for index in range(1, LANES // width)]
    return jnp.concatenate(parts, axis=0)


def ring(offset, size):
    return min(offset % size, -offset % size)


def far_first(pairs, distance):
    return sorted((p for p in pairs if any(p)), key=lambda p: (-distance(*p), p))


def kernel(
    n_grp,
    n_tile,
    base_velocity_in,
    viscosity_in,
    friction_in,
    friction_probe_in,
    pixel_los_in,
    pixel_weight_in,
    pixel_cell_in,
    pixel_count_in,
    panels,
    increment_out,
    probe_out,
    coef_out,
    base_velocity,
    viscosity,
    friction,
    friction_probe,
    pixel_los,
    pixel_weight,
    pixel_cell,
    pixel_count,
    ext,
    pack,
    side_r,
    side_l,
    slots_out,
    slots_in,
    coef,
    src,
    field,
    inc_stage,
    ext2,
    pack2,
    side2_r,
    side2_l,
    probe_stage,
    low_stage,
    column,
    panel_buf,
    part_in,
    sum_in,
    halo_send,
    halo_recv,
    halo2_send,
    halo2_recv,
    local_sem,
    many_send,
    many_recv,
):
    g = lax.axis_index("grp")
    t = lax.axis_index("tile")
    up = lax.rem(g + n_grp - 1, n_grp)
    down = lax.rem(g + 1, n_grp)
    left = lax.rem(t + n_tile - 1, n_tile)
    right = lax.rem(t + 1, n_tile)

    y_size = 4
    x_size = n_grp // y_size
    z_size = n_tile // 4
    x, y_hi = lax.div(g, y_size), lax.rem(g, y_size)
    z, y_lo, core = lax.div(t, 4), lax.rem(lax.div(t, 2), 2), lax.rem(t, 2)
    y = 2 * y_hi + y_lo

    def tile_peer(dz, flip):
        lo = 1 - y_lo if flip >= 2 else y_lo
        side = 1 - core if flip % 2 else core
        return (g, 4 * lax.rem(z + dz, z_size) + 2 * lo + side)

    def grp_peer(dx, dy):
        return (y_size * lax.rem(x + dx, x_size) + lax.rem(y_hi + dy, y_size), t)

    def plane_peer(dx, dy):
        there = lax.rem(y + dy, 2 * y_size)
        return (y_size * lax.rem(x + dx, x_size) + lax.div(there, 2), 4 * z + 2 * lax.rem(there, 2) + core)

    def line_peer(dz, flip):
        return (g, 4 * lax.rem(z + dz, z_size) + 2 * y_lo + (1 - core if flip else core))

    tile_offsets = far_first(
        [(dz, flip) for dz in range(z_size) for flip in range(4)], lambda dz, flip: ring(dz, z_size) + (flip >= 2)
    )
    grp_offsets = far_first(
        [(dx, dy) for dx in range(x_size) for dy in range(y_size)],
        lambda dx, dy: ring(dx, x_size) + 2 * ring(dy, y_size),
    )
    plane_offsets = far_first(
        [(dx, dy) for dx in range(x_size) for dy in range(2 * y_size)],
        lambda dx, dy: ring(dx, x_size) + ring(dy, 2 * y_size),
    )
    line_offsets = far_first(
        [(dz, flip) for dz in range(z_size) for flip in range(2)], lambda dz, flip: ring(dz, z_size)
    )

    barrier = pltpu.get_barrier_semaphore()
    corners = [(a, b) for a in (up, down) for b in (left, right)]
    across = [plane_peer(*p) for p in plane_offsets if p[1] % 2]
    peers = [grp_peer(*p) for p in grp_offsets] + corners + across + [tile_peer(*p) for p in tile_offsets if p != (0, 2)]
    for peer in peers:
        pl.semaphore_signal(barrier, inc=1, device_id=peer, device_id_type=MESH)

    loads = [
        pltpu.make_async_copy(a, b, local_sem.at[3 + index])
        for index, (a, b) in enumerate(
            [
                (base_velocity_in, base_velocity),
                (viscosity_in, viscosity),
                (friction_in, friction),
                (friction_probe_in, friction_probe),
                (pixel_los_in.at[0, 0], pixel_los),
                (pixel_weight_in.at[0, 0], pixel_weight),
                (pixel_cell_in.at[0, 0], pixel_cell),
                (pixel_count_in.at[0, 0], pixel_count),
            ]
        )
    ]
    for load in loads:
        load.start()

    panel_copy = pltpu.make_async_copy(panels, panel_buf, local_sem.at[0])
    panel_copy.start()

    for load in loads[:4]:
        load.wait()
    bvx = base_velocity[0]
    bvy = base_velocity[1]
    fp = friction_probe[...]
    own = (viscosity[...], friction[...], -(fp * bvx), -(fp * bvy))
    for index in range(4):
        ext[index, HALO : HALO + 64, :] = own[index]
    packed = pack_rims(own)
    pack[0:8] = packed[0:8]
    pack[8:40] = fold_rows(packed, 64)
    pack[40:48] = packed[56:64]

    for load in loads[4:]:
        load.wait()
    odd = lax.rem(t, 2)
    lane1 = lane_of((1, LANES))
    for pair in range(n_tile // 2):
        lanes = slice(pair * LANES, (pair + 1) * LANES)
        count = jnp.where(lane1 < CAP, pixel_count[0, 2 * pair], pixel_count[0, 2 * pair + 1])
        live = lax.rem(lane1, CAP) < count
        block = jnp.concatenate(
            [
                pixel_los[:, lanes],
                jnp.where(live, pixel_weight[:, lanes], 0.0),
                pixel_cell[:, lanes].astype(F32),
            ],
            axis=0,
        )
        slots_out[pair] = jnp.where(odd == 1, pltpu.roll(block, CAP, 1), block)

    pl.semaphore_wait(barrier, len(peers))

    def rim_copies(block, packed, from_right, from_left, send, recv):
        first, last = pl.ds(HALO, HALO), pl.ds(64, HALO)
        above, below = pl.ds(0, HALO), pl.ds(64 + HALO, HALO)
        high = packed.shape[0] - 16
        head, middle, tail = pl.ds(0, 8), pl.ds(8, high), pl.ds(8 + high, 8)
        moves = [
            (packed.at[head], from_right.at[tail], (up, left)),
            (packed.at[head], from_left.at[tail], (up, right)),
            (packed.at[tail], from_right.at[head], (down, left)),
            (packed.at[tail], from_left.at[head], (down, right)),
            (block.at[:, first], block.at[:, below], (up, t)),
            (block.at[:, last], block.at[:, above], (down, t)),
            (packed.at[middle], from_right.at[middle], (g, left)),
            (packed.at[middle], from_left.at[middle], (g, right)),
        ]
        return [
            pltpu.make_async_remote_copy(
                src_ref=a,
                dst_ref=b,
                send_sem=send.at[index],
                recv_sem=recv.at[index],
                device_id=target,
                device_id_type=MESH,
            )
            for index, (a, b, target) in enumerate(moves)
        ]

    def wait_bytes(ref, sem):
        pltpu.make_async_copy(ref, ref, sem).wait()

    copies = rim_copies(ext, pack, side_r, side_l, halo_send, halo_recv)
    for copy in copies:
        copy.start()

    for dz, flip in tile_offsets:
        peer = tile_peer(dz, flip)
        pltpu.make_async_remote_copy(
            src_ref=slots_out.at[lax.div(peer[1], 2)],
            dst_ref=slots_in.at[4 * dz + flip],
            send_sem=many_send.at[0],
            recv_sem=many_recv.at[0],
            device_id=peer,
            device_id_type=MESH,
        ).start()
    slots_in[0] = slots_out[lax.div(t, 2)]

    for copy in copies:
        copy.wait_recv()

    rows = 64 + 2 * HALO
    lane = lane_of((rows, LANES))
    row = row_of((rows, LANES))

    def widen(block, from_right, from_left):
        merged = jnp.where(lax.rem(lane_of(from_right.shape), 16) >= 8, from_right[...], from_left[...])
        high = merged.shape[0] - 16
        middle = unfold_rows(merged[8 : 8 + high], 2 * high)
        merged = jnp.concatenate([merged[0:8], middle, merged[8 + high :]], axis=0)
        fields = []
        for index in range(block.shape[0]):
            beside = pltpu.roll(merged, LANES - 16 * index - 8, 1)
            fields.append(jnp.concatenate([block[index], beside], axis=1))
        return fields

    v, fr, sx, sy = widen(ext, side_r, side_l)
    row_inside = ((row >= HALO) | (g > 0)) & ((row < HALO + 64) | (g < n_grp - 1))
    col_inside = ((lane < HALO) & (t < n_tile - 1)) | ((lane >= LANES - HALO) & (t > 0))
    inside = jnp.concatenate([row_inside, row_inside & col_inside], axis=1)
    v = jnp.where(inside, v, 0.0)
    pair_sum = v + row_next(v)
    east = 0.5 * pair_sum
    west = row_prev(east)
    north = 0.5 * (v + col_next(v))
    south = col_prev(north)
    node_pp = 0.0625 * (pair_sum + col_next(pair_sum))
    node_mp = row_prev(node_pp)
    node_pm = col_prev(node_pp)
    node_mm = col_prev(node_mp)
    diag_x = fr + 2.0 * (east + west) + (north + south)
    diag_y = fr + (east + west) + 2.0 * (north + south)
    inv_x = jnp.where(inside, RELAX / jnp.where(inside, diag_x, 1.0), 0.0)
    inv_y = jnp.where(inside, RELAX / jnp.where(inside, diag_y, 1.0), 0.0)
    for index, term in enumerate((east, west, north, south, node_pp, node_mp, node_pm, node_mm, inv_x, inv_y)):
        coef[index] = term
    src[0] = sx
    src[1] = sy

    def sweep(_, carry):
        cx, cy = field[0], field[1]
        ux, uy = row_next(cx), row_next(cy)
        dx, dy = row_prev(cx), row_prev(cy)
        e, w, n, s = coef[0], coef[1], coef[2], coef[3]
        pp, mp, pm, mm = coef[4], coef[5], coef[6], coef[7]
        ax = 2.0 * (e * ux + w * dx)
        ax += col_next(s * cx + (pm * uy - mm * dy))
        ax += col_prev(n * cx + (mp * dy - pp * uy))
        ay = e * uy + w * dy
        ay += col_next(2.0 * (s * cy) + (pm * ux - mm * dx))
        ay += col_prev(2.0 * (n * cy) + (mp * dx - pp * ux))
        field[0] = (1.0 - RELAX) * cx + coef[8] * (src[0] + ax)
        field[1] = (1.0 - RELAX) * cy + coef[9] * (src[1] + ay)
        return carry

    def relax():
        field[0] = coef[8] * src[0]
        field[1] = coef[9] * src[1]
        lax.fori_loop(1, SWEEPS, sweep, 0)
        return field[0, HALO : HALO + 64, :LANES], field[1, HALO : HALO + 64, :LANES]

    inc_x, inc_y = relax()
    inc_stage[0] = inc_x
    inc_stage[1] = inc_y
    increment_copy = pltpu.make_async_copy(inc_stage, increment_out, local_sem.at[1])
    increment_copy.start()

    wait_bytes(slots_in.at[pl.ds(0, n_tile - 1)], many_recv.at[0])

    def halves(a):
        high = a.astype(BF16)
        return high, (a - high.astype(F32)).astype(BF16)

    xh, xl = halves(inc_x)
    yh, yl = halves(inc_y)
    stacked = jnp.concatenate([xh, yh, xl, yl], axis=0)
    chunk = 2 * LANES
    total = jnp.zeros((256, LANES), F32)
    low_half = lane_of((4, LANES)) < CAP
    for index in range(n_tile * CAP // chunk):
        first = jnp.where(low_half, slots_in[4 * index], slots_in[4 * index + 1])
        second = jnp.where(low_half, slots_in[4 * index + 2], slots_in[4 * index + 3])
        lists = jnp.concatenate([first, second], axis=1)
        los_x, los_y, weight = lists[0:1], lists[1:2], lists[2:3]
        cell = lists[3:4].astype(jnp.int32)
        at_col = row_of((LANES, chunk)) == (cell & (LANES - 1))
        at_row = row_of((64, chunk)) == (cell >> 7)
        col_hot = jnp.where(at_col, 1.0, 0.0).astype(BF16)
        found = jnp.dot(stacked, col_hot, preferred_element_type=F32)
        got_x = jnp.sum(jnp.where(at_row, found[0:64] + found[128:192], 0.0), axis=0, keepdims=True)
        got_y = jnp.sum(jnp.where(at_row, found[64:128] + found[192:256], 0.0), axis=0, keepdims=True)
        amount = weight * (los_x * got_x + los_y * got_y)
        scaled = []
        for value in (amount * los_x, amount * los_y):
            high = value.astype(BF16).astype(F32)
            scaled.append((high, value - high))
        hot = [
            jnp.where(at_row, jnp.broadcast_to(part, (64, chunk)), 0.0)
            for part in (scaled[0][0], scaled[1][0], scaled[0][1], scaled[1][1])
        ]
        hot = jnp.concatenate(hot, axis=0).astype(BF16)
        total += lax.dot_general(hot, col_hot, (((1,), (1,)), ((), ())), preferred_element_type=F32)
    adjoint = (total[0:64] + total[128:192], total[64:128] + total[192:256])

    for index in range(2):
        ext2[index, HALO : HALO + 64, :] = adjoint[index]
    packed2 = pack_rims(adjoint)
    pack2[0:8] = packed2[0:8]
    pack2[8:24] = fold_rows(packed2, 32)
    pack2[24:32] = packed2[56:64]
    copies2 = rim_copies(ext2, pack2, side2_r, side2_l, halo2_send, halo2_recv)
    for copy in copies2:
        copy.start()
    for copy in copies2:
        copy.wait_recv()
    sx2, sy2 = widen(ext2, side2_r, side2_l)
    src[0] = sx2
    src[1] = sy2
    mult_x, mult_y = relax()

    probe = -(base_velocity[0] * mult_x + base_velocity[1] * mult_y)
    probe_low = probe.astype(BF16)
    low_stage[...] = probe_low
    column[g] = probe_low

    for offset in grp_offsets:
        pltpu.make_async_remote_copy(
            src_ref=low_stage,
            dst_ref=column.at[g],
            send_sem=many_send.at[1],
            recv_sem=many_recv.at[1],
            device_id=grp_peer(*offset),
            device_id_type=MESH,
        ).start()
    probe_stage[...] = probe
    probe_copy = pltpu.make_async_copy(probe_stage, probe_out, local_sem.at[2])
    probe_copy.start()
    panel_copy.wait()
    wait_bytes(column.at[pl.ds(0, n_grp - 1)], many_recv.at[1])

    def project(block, sums):
        values = column[block].astype(F32)
        start = pl.multiple_of(block * 64, 64)
        return tuple(
            total + jnp.sum((panel_buf[k, pl.ds(start, 64), :].astype(F32) * values).reshape(8, 8, LANES), axis=0)
            for k, total in enumerate(sums)
        )

    sums = lax.fori_loop(0, n_grp, project, tuple(jnp.zeros((8, LANES), F32) for _ in range(8)))
    partial = jnp.concatenate([jnp.sum(s, axis=0, keepdims=True) for s in sums], axis=0)
    partial = jnp.sum(partial, axis=1, keepdims=True)
    mine = lane_of((8, LANES)) == 8 * g + row_of((8, LANES))
    placed = jnp.sum(jnp.where(mine, jnp.broadcast_to(partial, (8, LANES)), 0.0), axis=0, keepdims=True)

    def sum_over(value, landing, offsets, peer, index):
        landing[0] = value
        for slot, offset in enumerate(offsets, 1):
            pltpu.make_async_remote_copy(
                src_ref=landing.at[0],
                dst_ref=landing.at[slot],
                send_sem=many_send.at[index],
                recv_sem=many_recv.at[index],
                device_id=peer(*offset),
                device_id_type=MESH,
            ).start()
        wait_bytes(landing.at[pl.ds(1, len(offsets))], many_recv.at[index])
        return jnp.sum(landing[...], axis=0)

    plane_sum = sum_over(placed, part_in, plane_offsets, plane_peer, 2)
    coef_out[...] = sum_over(plane_sum, sum_in, line_offsets, line_peer, 3)

    for copy in copies + copies2:
        copy.wait_send()
    wait_bytes(slots_in.at[pl.ds(0, n_tile - 1)], many_send.at[0])
    wait_bytes(column.at[pl.ds(0, n_grp - 1)], many_send.at[1])
    wait_bytes(part_in.at[pl.ds(1, len(plane_offsets))], many_send.at[2])
    wait_bytes(sum_in.at[pl.ds(1, len(line_offsets))], many_send.at[3])
    increment_copy.wait()
    probe_copy.wait()


def on_device(n_grp, n_tile, base_velocity, viscosity, friction, friction_probe, pixel_los, pixel_weight, pixel_cell, pixel_count, panels):
    slots = pixel_los.shape[-1]
    panel_rows = panels.shape[1]
    vmem = pl.BlockSpec(memory_space=pltpu.VMEM)
    hbm = pl.BlockSpec(memory_space=pltpu.HBM)
    wide = 64 + 2 * HALO
    increment, probe, coefficients = pl.pallas_call(
        functools.partial(kernel, n_grp, n_tile),
        out_shape=(
            jax.ShapeDtypeStruct((2, 64, LANES), F32),
            jax.ShapeDtypeStruct((64, LANES), F32),
            jax.ShapeDtypeStruct((1, LANES), F32),
        ),
        in_specs=[hbm] * 9,
        out_specs=(hbm, hbm, vmem),
        scratch_shapes=[
            pltpu.VMEM((2, 64, LANES), F32),
            pltpu.VMEM((64, LANES), F32),
            pltpu.VMEM((64, LANES), F32),
            pltpu.VMEM((64, LANES), F32),
            pltpu.VMEM((2, slots), F32),
            pltpu.VMEM((1, slots), F32),
            pltpu.VMEM((1, slots), jnp.int32),
            pltpu.SMEM((1, n_tile), jnp.int32),
            pltpu.VMEM((4, wide, LANES), F32),
            pltpu.VMEM((48, LANES), F32),
            pltpu.VMEM((48, LANES), F32),
            pltpu.VMEM((48, LANES), F32),
            pltpu.VMEM((n_tile // 2, 4, LANES), F32),
            pltpu.VMEM((n_tile, 4, LANES), F32),
            pltpu.VMEM((10, wide, 2 * LANES), F32),
            pltpu.VMEM((2, wide, 2 * LANES), F32),
            pltpu.VMEM((2, wide, 2 * LANES), F32),
            pltpu.VMEM((2, 64, LANES), F32),
            pltpu.VMEM((2, wide, LANES), F32),
            pltpu.VMEM((32, LANES), F32),
            pltpu.VMEM((32, LANES), F32),
            pltpu.VMEM((32, LANES), F32),
            pltpu.VMEM((64, LANES), F32),
            pltpu.VMEM((64, LANES), BF16),
            pltpu.VMEM((n_grp, 64, LANES), BF16),
            pltpu.VMEM((8, panel_rows, LANES), BF16),
            pltpu.VMEM((2 * n_grp, 1, LANES), F32),
            pltpu.VMEM((n_tile // 2, 1, LANES), F32),
            pltpu.SemaphoreType.DMA((8,)),
            pltpu.SemaphoreType.DMA((8,)),
            pltpu.SemaphoreType.DMA((8,)),
            pltpu.SemaphoreType.DMA((8,)),
            pltpu.SemaphoreType.DMA((11,)),
            pltpu.SemaphoreType.DMA((4,)),
            pltpu.SemaphoreType.DMA((4,)),
        ],
        compiler_params=pltpu.CompilerParams(
            collective_id=0, has_side_effects=True, vmem_limit_bytes=60 * 1024 * 1024
        ),
    )(
        base_velocity,
        viscosity,
        friction,
        friction_probe,
        pixel_los,
        pixel_weight,
        pixel_cell,
        pixel_count,
        panels,
    )
    return increment, probe, coefficients.reshape(LANES)[: 8 * n_grp]


def solution(mesh):
    in_specs = (
        P(None, "grp", "tile"),
        P("grp", "tile"),
        P("grp", "tile"),
        P("grp", "tile"),
        P("grp", "tile", None, None),
        P("grp", "tile", None, None),
        P("grp", "tile", None, None),
        P("grp", "tile", None, None),
        P("grp", None, "tile"),
    )
    out_specs = (P(None, "grp", "tile"), P("grp", "tile"), P())
    body = functools.partial(on_device, mesh.shape["grp"], mesh.shape["tile"])
    return jax.shard_map(body, mesh=mesh, in_specs=in_specs, out_specs=out_specs, check_vma=False)
```

```python
import functools

import jax
import jax.numpy as jnp
from jax import lax
from jax.experimental import pallas as pl
from jax.experimental.pallas import tpu as pltpu
from jax.sharding import PartitionSpec as P

SWEEPS = 8
RELAX = 0.8
HALO = 8
CAP = 64
LANES = 128
MESH = pl.DeviceIdType.MESH
F32 = jnp.float32
BF16 = jnp.bfloat16


def lane_of(shape):
    return lax.broadcasted_iota(jnp.int32, shape, 1)


def row_of(shape):
    return lax.broadcasted_iota(jnp.int32, shape, 0)


def row_next(a):
    return pltpu.roll(a, a.shape[0] - 1, 0)


def row_prev(a):
    return pltpu.roll(a, 1, 0)


def col_next(a):
    return pltpu.roll(a, a.shape[1] - 1, 1)


def col_prev(a):
    return pltpu.roll(a, 1, 1)


def pack_rims(fields):
    lane = lane_of(fields[0].shape)
    packed = pltpu.roll(fields[0], 8, 1)
    for index, field in enumerate(fields[1:], 1):
        moved = pltpu.roll(field, 16 * index + 8, 1)
        packed = jnp.where(lane >= 16 * index, moved, packed)
    return packed


def fold_rows(packed, width):
    high = width // 2
    folded = packed[0:high]
    lane = lane_of(folded.shape)
    for index in range(1, LANES // width):
        moved = pltpu.roll(packed[index * high : (index + 1) * high], index * width, 1)
        folded = jnp.where(lane >= index * width, moved, folded)
    return folded


def unfold_rows(folded, width):
    parts = [folded] + [pltpu.roll(folded, LANES - index * width, 1) for index in range(1, LANES // width)]
    return jnp.concatenate(parts, axis=0)


def ring(offset, size):
    return min(offset % size, -offset % size)


def far_first(pairs, distance):
    return sorted((p for p in pairs if any(p)), key=lambda p: (-distance(*p), p))


def kernel(
    n_grp,
    n_tile,
    base_velocity_in,
    viscosity_in,
    friction_in,
    friction_probe_in,
    pixel_los_in,
    pixel_weight_in,
    pixel_cell_in,
    pixel_count_in,
    panels,
    increment_out,
    probe_out,
    coef_out,
    base_velocity,
    viscosity,
    friction,
    friction_probe,
    pixel_los,
    pixel_weight,
    pixel_cell,
    pixel_count,
    ext,
    pack,
    side_r,
    side_l,
    slots_out,
    slots_in,
    coef,
    src,
    field,
    inc_stage,
    ext2,
    pack2,
    side2_r,
    side2_l,
    probe_stage,
    early_stage,
    early_in,
    late_stage,
    late_in,
    column,
    panel_buf,
    panel_ext,
    panel_rim,
    part_in,
    sum_in,
    halo_send,
    halo_recv,
    halo2_send,
    halo2_recv,
    rim_send,
    rim_recv,
    local_sem,
    many_send,
    many_recv,
):
    g = lax.axis_index("grp")
    t = lax.axis_index("tile")
    up = lax.rem(g + n_grp - 1, n_grp)
    down = lax.rem(g + 1, n_grp)
    left = lax.rem(t + n_tile - 1, n_tile)
    right = lax.rem(t + 1, n_tile)

    y_size = 4
    x_size = n_grp // y_size
    z_size = n_tile // 4
    x, y_hi = lax.div(g, y_size), lax.rem(g, y_size)
    z, y_lo, core = lax.div(t, 4), lax.rem(lax.div(t, 2), 2), lax.rem(t, 2)
    y = 2 * y_hi + y_lo

    def tile_peer(dz, flip):
        lo = 1 - y_lo if flip >= 2 else y_lo
        side = 1 - core if flip % 2 else core
        return (g, 4 * lax.rem(z + dz, z_size) + 2 * lo + side)

    def grp_peer(dx, dy):
        return (y_size * lax.rem(x + dx, x_size) + lax.rem(y_hi + dy, y_size), t)

    def plane_peer(dx, dy):
        there = lax.rem(y + dy, 2 * y_size)
        return (y_size * lax.rem(x + dx, x_size) + lax.div(there, 2), 4 * z + 2 * lax.rem(there, 2) + core)

    def line_peer(dz, flip):
        return (g, 4 * lax.rem(z + dz, z_size) + 2 * y_lo + (1 - core if flip else core))

    tile_offsets = far_first(
        [(dz, flip) for dz in range(z_size) for flip in range(4)], lambda dz, flip: ring(dz, z_size) + (flip >= 2)
    )
    grp_offsets = far_first(
        [(dx, dy) for dx in range(x_size) for dy in range(y_size)],
        lambda dx, dy: ring(dx, x_size) + 2 * ring(dy, y_size),
    )
    plane_offsets = far_first(
        [(dx, dy) for dx in range(x_size) for dy in range(2 * y_size)],
        lambda dx, dy: ring(dx, x_size) + ring(dy, 2 * y_size),
    )
    line_offsets = far_first(
        [(dz, flip) for dz in range(z_size) for flip in range(2)], lambda dz, flip: ring(dz, z_size)
    )

    barrier = pltpu.get_barrier_semaphore()
    corners = [(a, b) for a in (up, down) for b in (left, right)]
    across = [plane_peer(*p) for p in plane_offsets if p[1] % 2]
    peers = corners + [(up, t), (down, t), (g, left), (g, right)]
    peers += [grp_peer(*p) for p in grp_offsets] + across + [tile_peer(*p) for p in tile_offsets if p != (0, 2)]
    for peer in peers:
        pl.semaphore_signal(barrier, inc=1, device_id=peer, device_id_type=MESH)

    loads = [
        pltpu.make_async_copy(a, b, local_sem.at[3 + index])
        for index, (a, b) in enumerate(
            [
                (base_velocity_in, base_velocity.at[:, pl.ds(HALO, 64)]),
                (viscosity_in, viscosity),
                (friction_in, friction),
                (friction_probe_in, friction_probe),
                (pixel_los_in.at[0, 0], pixel_los),
                (pixel_weight_in.at[0, 0], pixel_weight),
                (pixel_cell_in.at[0, 0], pixel_cell),
                (pixel_count_in.at[0, 0], pixel_count),
            ]
        )
    ]
    for load in loads:
        load.start()

    panel_copy = pltpu.make_async_copy(panels, panel_buf, local_sem.at[0])
    panel_copy.start()

    for load in loads[:4]:
        load.wait()
    bvx = base_velocity[0, HALO : HALO + 64]
    bvy = base_velocity[1, HALO : HALO + 64]
    fp = friction_probe[...]
    own = (viscosity[...], friction[...], -(fp * bvx), -(fp * bvy))
    for index in range(4):
        ext[index, HALO : HALO + 64, :] = own[index]
    packed = pack_rims(own)
    pack[0:8] = packed[0:8]
    pack[8:40] = fold_rows(packed, 64)
    pack[40:48] = packed[56:64]

    for load in loads[4:]:
        load.wait()
    odd = lax.rem(t, 2)
    lane1 = lane_of((1, LANES))
    for pair in range(n_tile // 2):
        lanes = slice(pair * LANES, (pair + 1) * LANES)
        count = jnp.where(lane1 < CAP, pixel_count[0, 2 * pair], pixel_count[0, 2 * pair + 1])
        live = lax.rem(lane1, CAP) < count
        block = jnp.concatenate(
            [
                pixel_los[:, lanes],
                jnp.where(live, pixel_weight[:, lanes], 0.0),
                pixel_cell[:, lanes].astype(F32),
            ],
            axis=0,
        )
        slots_out[pair] = jnp.where(odd == 1, pltpu.roll(block, CAP, 1), block)

    pl.semaphore_wait(barrier, len(peers))

    def remote(src_ref, dst_ref, send_sem, recv_sem, peer):
        return pltpu.make_async_remote_copy(
            src_ref=src_ref,
            dst_ref=dst_ref,
            send_sem=send_sem,
            recv_sem=recv_sem,
            device_id=peer,
            device_id_type=MESH,
        )

    def rim_copies(block, packed, from_right, from_left, send, recv):
        first, last = pl.ds(HALO, HALO), pl.ds(64, HALO)
        above, below = pl.ds(0, HALO), pl.ds(64 + HALO, HALO)
        high = packed.shape[0] - 16
        head, middle, tail = pl.ds(0, 8), pl.ds(8, high), pl.ds(8 + high, 8)
        moves = [
            (packed.at[head], from_right.at[tail], (up, left)),
            (packed.at[head], from_left.at[tail], (up, right)),
            (packed.at[tail], from_right.at[head], (down, left)),
            (packed.at[tail], from_left.at[head], (down, right)),
            (block.at[:, first], block.at[:, below], (up, t)),
            (block.at[:, last], block.at[:, above], (down, t)),
            (packed.at[middle], from_right.at[middle], (g, left)),
            (packed.at[middle], from_left.at[middle], (g, right)),
        ]
        return [remote(a, b, send.at[index], recv.at[index], peer) for index, (a, b, peer) in enumerate(moves)]

    def wait_bytes(ref, sem):
        pltpu.make_async_copy(ref, ref, sem).wait()

    copies = rim_copies(ext, pack, side_r, side_l, halo_send, halo_recv)
    for copy in copies:
        copy.start()
    first, last = pl.ds(HALO, HALO), pl.ds(64, HALO)
    above, below = pl.ds(0, HALO), pl.ds(64 + HALO, HALO)
    velocity_rims = [
        remote(base_velocity.at[:, first], base_velocity.at[:, below], rim_send.at[0], rim_recv.at[0], (up, t)),
        remote(base_velocity.at[:, last], base_velocity.at[:, above], rim_send.at[1], rim_recv.at[1], (down, t)),
    ]
    for copy in velocity_rims:
        copy.start()

    for dz, flip in tile_offsets:
        peer = tile_peer(dz, flip)
        remote(
            slots_out.at[lax.div(peer[1], 2)], slots_in.at[4 * dz + flip], many_send.at[0], many_recv.at[0], peer
        ).start()
    slots_in[0] = slots_out[lax.div(t, 2)]

    for copy in copies:
        copy.wait_recv()

    rows = 64 + 2 * HALO
    lane = lane_of((rows, LANES))
    row = row_of((rows, LANES))

    def merge(from_right, from_left):
        return jnp.where(lax.rem(lane_of(from_right.shape), 16) >= 8, from_right, from_left)

    def beside(merged, index):
        return pltpu.roll(merged, LANES - 16 * index - 8, 1)

    def widen(block, from_right, from_left):
        merged = merge(from_right[...], from_left[...])
        high = merged.shape[0] - 16
        middle = unfold_rows(merged[8 : 8 + high], 2 * high)
        merged = jnp.concatenate([merged[0:8], middle, merged[8 + high :]], axis=0)
        return [
            jnp.concatenate([block[index], beside(merged, index)], axis=1) for index in range(block.shape[0])
        ]

    v, fr, sx, sy = widen(ext, side_r, side_l)
    row_inside = ((row >= HALO) | (g > 0)) & ((row < HALO + 64) | (g < n_grp - 1))
    col_inside = ((lane < HALO) & (t < n_tile - 1)) | ((lane >= LANES - HALO) & (t > 0))
    inside = jnp.concatenate([row_inside, row_inside & col_inside], axis=1)
    v = jnp.where(inside, v, 0.0)
    pair_sum = v + row_next(v)
    east = 0.5 * pair_sum
    west = row_prev(east)
    north = 0.5 * (v + col_next(v))
    south = col_prev(north)
    node_pp = 0.0625 * (pair_sum + col_next(pair_sum))
    node_mp = row_prev(node_pp)
    node_pm = col_prev(node_pp)
    node_mm = col_prev(node_mp)
    diag_x = fr + 2.0 * (east + west) + (north + south)
    diag_y = fr + (east + west) + 2.0 * (north + south)
    inv_x = jnp.where(inside, RELAX / jnp.where(inside, diag_x, 1.0), 0.0)
    inv_y = jnp.where(inside, RELAX / jnp.where(inside, diag_y, 1.0), 0.0)
    for index, term in enumerate((east, west, north, south, node_pp, node_mp, node_pm, node_mm, inv_x, inv_y)):
        coef[index] = term
    src[0] = sx
    src[1] = sy

    def sweep(_, carry):
        cx, cy = field[0], field[1]
        ux, uy = row_next(cx), row_next(cy)
        dx, dy = row_prev(cx), row_prev(cy)
        e, w, n, s = coef[0], coef[1], coef[2], coef[3]
        pp, mp, pm, mm = coef[4], coef[5], coef[6], coef[7]
        ax = 2.0 * (e * ux + w * dx)
        ax += col_next(s * cx + (pm * uy - mm * dy))
        ax += col_prev(n * cx + (mp * dy - pp * uy))
        ay = e * uy + w * dy
        ay += col_next(2.0 * (s * cy) + (pm * ux - mm * dx))
        ay += col_prev(2.0 * (n * cy) + (mp * dx - pp * ux))
        field[0] = (1.0 - RELAX) * cx + coef[8] * (src[0] + ax)
        field[1] = (1.0 - RELAX) * cy + coef[9] * (src[1] + ay)
        return carry

    def relax():
        field[0] = coef[8] * src[0]
        field[1] = coef[9] * src[1]
        lax.fori_loop(1, SWEEPS, sweep, 0)

    def probe_of(at):
        return -(base_velocity[0, at] * field[0, at, :LANES] + base_velocity[1, at] * field[1, at, :LANES])

    own_rows = slice(HALO, HALO + 64)
    relax()
    inc_x, inc_y = field[0, own_rows, :LANES], field[1, own_rows, :LANES]
    inc_stage[0] = inc_x
    inc_stage[1] = inc_y
    increment_copy = pltpu.make_async_copy(inc_stage, increment_out, local_sem.at[1])
    increment_copy.start()

    wait_bytes(slots_in.at[pl.ds(0, n_tile - 1)], many_recv.at[0])

    def halves(a):
        high = a.astype(BF16)
        return high, (a - high.astype(F32)).astype(BF16)

    xh, xl = halves(inc_x)
    yh, yl = halves(inc_y)
    stacked = jnp.concatenate([xh, yh, xl, yl], axis=0)
    chunk = 2 * LANES
    total = jnp.zeros((256, LANES), F32)
    low_half = lane_of((4, LANES)) < CAP
    for index in range(n_tile * CAP // chunk):
        first = jnp.where(low_half, slots_in[4 * index], slots_in[4 * index + 1])
        second = jnp.where(low_half, slots_in[4 * index + 2], slots_in[4 * index + 3])
        lists = jnp.concatenate([first, second], axis=1)
        los_x, los_y, weight = lists[0:1], lists[1:2], lists[2:3]
        cell = lists[3:4].astype(jnp.int32)
        at_col = row_of((LANES, chunk)) == (cell & (LANES - 1))
        at_row = row_of((64, chunk)) == (cell >> 7)
        col_hot = jnp.where(at_col, 1.0, 0.0).astype(BF16)
        found = jnp.dot(stacked, col_hot, preferred_element_type=F32)
        got_x = jnp.sum(jnp.where(at_row, found[0:64] + found[128:192], 0.0), axis=0, keepdims=True)
        got_y = jnp.sum(jnp.where(at_row, found[64:128] + found[192:256], 0.0), axis=0, keepdims=True)
        amount = weight * (los_x * got_x + los_y * got_y)
        scaled = []
        for value in (amount * los_x, amount * los_y):
            high = value.astype(BF16).astype(F32)
            scaled.append((high, value - high))
        hot = [
            jnp.where(at_row, jnp.broadcast_to(part, (64, chunk)), 0.0)
            for part in (scaled[0][0], scaled[1][0], scaled[0][1], scaled[1][1])
        ]
        hot = jnp.concatenate(hot, axis=0).astype(BF16)
        total += lax.dot_general(hot, col_hot, (((1,), (1,)), ((), ())), preferred_element_type=F32)
    adjoint = (total[0:64] + total[128:192], total[64:128] + total[192:256])

    for index in range(2):
        ext2[index, HALO : HALO + 64, :] = adjoint[index]
    packed2 = pack_rims(adjoint)
    pack2[0:8] = packed2[0:8]
    pack2[8:24] = fold_rows(packed2, 32)
    pack2[24:32] = packed2[56:64]
    copies2 = rim_copies(ext2, pack2, side2_r, side2_l, halo2_send, halo2_recv)
    for copy in copies2[6:] + copies2[:6]:
        copy.start()

    for index in range(2):
        src[index] = jnp.zeros((rows, 2 * LANES), F32)
        src[index, own_rows, :LANES] = adjoint[index]
    relax()
    for copy in velocity_rims:
        copy.wait_recv()
    everything = slice(0, rows)
    part = probe_of(everything).astype(BF16)
    early_stage[...] = part
    early_in[g] = part
    for offset in grp_offsets:
        remote(early_stage, early_in.at[g], many_send.at[1], many_recv.at[1], grp_peer(*offset)).start()

    panel_copy.wait()
    panel_ext[0:HALO] = jnp.zeros((HALO, LANES), F32)
    panel_ext[HALO + 64 * n_grp :] = jnp.zeros((HALO, LANES), F32)
    fold_lane = lane_of((16, LANES))

    def fold_late(block, start):
        folded = jnp.zeros((16, LANES), F32)
        for j in range(rows // 16):
            moved = pltpu.roll(block[start + 16 * j : start + 16 * j + 16, :], 16 * j + 8, 1)
            here = (fold_lane >= 16 * j) & (fold_lane < 16 * j + 16)
            folded = jnp.where(here, moved, folded)
        return folded

    def fold_panel(k, carry):
        panel_ext[HALO : HALO + 64 * n_grp] = panel_buf[k].astype(F32)
        for block in range(n_grp):
            panel_rim[k, block] = fold_late(panel_ext, 64 * block)
        return carry

    lax.fori_loop(0, 8, fold_panel, 0)

    for copy in copies2[6:]:
        copy.wait_recv()
    middle = unfold_rows(merge(side2_r[8:24], side2_l[8:24]), 32)
    for index in range(2):
        src[index, own_rows, LANES:] = beside(middle, index)
    relax()
    late = fold_late(probe_of(everything), 0).astype(BF16)
    late_stage[...] = late
    late_in[g] = late
    for offset in grp_offsets:
        remote(late_stage, late_in.at[g], many_send.at[2], many_recv.at[2], grp_peer(*offset)).start()

    for copy in copies2[:6]:
        copy.wait_recv()
    for at, edge in ((slice(0, 8), slice(0, 8)), (slice(64 + HALO, rows), slice(24, 32))):
        merged = merge(side2_r[edge], side2_l[edge])
        for index in range(2):
            src[index, at, :LANES] = ext2[index, at]
            src[index, at, LANES:] = beside(merged, index)
    relax()
    probe_stage[...] = probe_of(own_rows)
    probe_copy = pltpu.make_async_copy(probe_stage, probe_out, local_sem.at[2])
    probe_copy.start()

    wait_bytes(early_in.at[pl.ds(0, n_grp - 1)], many_recv.at[1])
    column[...] = jnp.zeros_like(column)
    part_lane = lane_of((rows, LANES))
    is_middle = (part_lane >= HALO) & (part_lane < LANES - HALO)
    for block in range(n_grp):
        at = slice(64 * block, 64 * block + rows)
        column[at] += jnp.where(is_middle, early_in[block].astype(F32), 0.0)

    def project(block, sums):
        start = pl.multiple_of(block * 64, 64)
        values = column[pl.ds(start + HALO, 64), :]
        return tuple(
            total + jnp.sum((panel_buf[k, pl.ds(start, 64), :].astype(F32) * values).reshape(8, 8, LANES), axis=0)
            for k, total in enumerate(sums)
        )

    sums = lax.fori_loop(0, n_grp, project, tuple(jnp.zeros((8, LANES), F32) for _ in range(8)))
    wait_bytes(late_in.at[pl.ds(0, n_grp - 1)], many_recv.at[2])
    sums = list(sums)
    for block in range(n_grp):
        late = late_in[block].astype(F32)
        for k in range(8):
            product = panel_rim[k, block] * late
            sums[k] = sums[k] + product[0:8] + product[8:16]
    partial = jnp.concatenate([jnp.sum(s, axis=0, keepdims=True) for s in sums], axis=0)
    partial = jnp.sum(partial, axis=1, keepdims=True)
    mine = lane_of((8, LANES)) == 8 * g + row_of((8, LANES))
    placed = jnp.sum(jnp.where(mine, jnp.broadcast_to(partial, (8, LANES)), 0.0), axis=0, keepdims=True)

    def sum_over(value, landing, offsets, peer, index):
        landing[0] = value
        for slot, offset in enumerate(offsets, 1):
            remote(
                landing.at[0], landing.at[slot], many_send.at[index], many_recv.at[index], peer(*offset)
            ).start()
        wait_bytes(landing.at[pl.ds(1, len(offsets))], many_recv.at[index])
        return jnp.sum(landing[...], axis=0)

    plane_sum = sum_over(placed, part_in, plane_offsets, plane_peer, 3)
    coef_out[...] = sum_over(plane_sum, sum_in, line_offsets, line_peer, 4)

    for copy in copies + velocity_rims + copies2:
        copy.wait_send()
    wait_bytes(slots_in.at[pl.ds(0, n_tile - 1)], many_send.at[0])
    wait_bytes(early_in.at[pl.ds(0, n_grp - 1)], many_send.at[1])
    wait_bytes(late_in.at[pl.ds(0, n_grp - 1)], many_send.at[2])
    wait_bytes(part_in.at[pl.ds(1, len(plane_offsets))], many_send.at[3])
    wait_bytes(sum_in.at[pl.ds(1, len(line_offsets))], many_send.at[4])
    increment_copy.wait()
    probe_copy.wait()


def on_device(n_grp, n_tile, base_velocity, viscosity, friction, friction_probe, pixel_los, pixel_weight, pixel_cell, pixel_count, panels):
    slots = pixel_los.shape[-1]
    panel_rows = panels.shape[1]
    vmem = pl.BlockSpec(memory_space=pltpu.VMEM)
    hbm = pl.BlockSpec(memory_space=pltpu.HBM)
    wide = 64 + 2 * HALO
    increment, probe, coefficients = pl.pallas_call(
        functools.partial(kernel, n_grp, n_tile),
        out_shape=(
            jax.ShapeDtypeStruct((2, 64, LANES), F32),
            jax.ShapeDtypeStruct((64, LANES), F32),
            jax.ShapeDtypeStruct((1, LANES), F32),
        ),
        in_specs=[hbm] * 9,
        out_specs=(hbm, hbm, vmem),
        scratch_shapes=[
            pltpu.VMEM((2, wide, LANES), F32),
            pltpu.VMEM((64, LANES), F32),
            pltpu.VMEM((64, LANES), F32),
            pltpu.VMEM((64, LANES), F32),
            pltpu.VMEM((2, slots), F32),
            pltpu.VMEM((1, slots), F32),
            pltpu.VMEM((1, slots), jnp.int32),
            pltpu.SMEM((1, n_tile), jnp.int32),
            pltpu.VMEM((4, wide, LANES), F32),
            pltpu.VMEM((48, LANES), F32),
            pltpu.VMEM((48, LANES), F32),
            pltpu.VMEM((48, LANES), F32),
            pltpu.VMEM((n_tile // 2, 4, LANES), F32),
            pltpu.VMEM((n_tile, 4, LANES), F32),
            pltpu.VMEM((10, wide, 2 * LANES), F32),
            pltpu.VMEM((2, wide, 2 * LANES), F32),
            pltpu.VMEM((2, wide, 2 * LANES), F32),
            pltpu.VMEM((2, 64, LANES), F32),
            pltpu.VMEM((2, wide, LANES), F32),
            pltpu.VMEM((32, LANES), F32),
            pltpu.VMEM((32, LANES), F32),
            pltpu.VMEM((32, LANES), F32),
            pltpu.VMEM((64, LANES), F32),
            pltpu.VMEM((wide, LANES), BF16),
            pltpu.VMEM((n_grp, wide, LANES), BF16),
            pltpu.VMEM((16, LANES), BF16),
            pltpu.VMEM((n_grp, 16, LANES), BF16),
            pltpu.VMEM((panel_rows + 2 * HALO, LANES), F32),
            pltpu.VMEM((8, panel_rows, LANES), BF16),
            pltpu.VMEM((panel_rows + 2 * HALO, LANES), F32),
            pltpu.VMEM((8, n_grp, 16, LANES), F32),
            pltpu.VMEM((2 * n_grp, 1, LANES), F32),
            pltpu.VMEM((n_tile // 2, 1, LANES), F32),
            pltpu.SemaphoreType.DMA((8,)),
            pltpu.SemaphoreType.DMA((8,)),
            pltpu.SemaphoreType.DMA((8,)),
            pltpu.SemaphoreType.DMA((8,)),
            pltpu.SemaphoreType.DMA((2,)),
            pltpu.SemaphoreType.DMA((2,)),
            pltpu.SemaphoreType.DMA((11,)),
            pltpu.SemaphoreType.DMA((5,)),
            pltpu.SemaphoreType.DMA((5,)),
        ],
        compiler_params=pltpu.CompilerParams(
            collective_id=0, has_side_effects=True, vmem_limit_bytes=24 * 1024 * 1024
        ),
    )(
        *(
            pltpu.with_memory_space_constraint(a, pltpu.HBM)
            for a in (
                base_velocity,
                viscosity,
                friction,
                friction_probe,
                pixel_los,
                pixel_weight,
                pixel_cell,
                pixel_count,
                panels,
            )
        )
    )
    return increment, probe, coefficients.reshape(LANES)[: 8 * n_grp]


def solution(mesh):
    in_specs = (
        P(None, "grp", "tile"),
        P("grp", "tile"),
        P("grp", "tile"),
        P("grp", "tile"),
        P("grp", "tile", None, None),
        P("grp", "tile", None, None),
        P("grp", "tile", None, None),
        P("grp", "tile", None, None),
        P("grp", None, "tile"),
    )
    out_specs = (P(None, "grp", "tile"), P("grp", "tile"), P())
    body = functools.partial(on_device, mesh.shape["grp"], mesh.shape["tile"])
    return jax.shard_map(body, mesh=mesh, in_specs=in_specs, out_specs=out_specs, check_vma=False)
```

```python
import functools

import jax
import jax.numpy as jnp
from jax import lax
from jax.experimental import pallas as pl
from jax.experimental.pallas import tpu as pltpu
from jax.sharding import PartitionSpec as P

SWEEPS = 8
RELAX = 0.8
HALO = 8
CAP = 64
LANES = 128
MESH = pl.DeviceIdType.MESH
F32 = jnp.float32
BF16 = jnp.bfloat16


def lane_of(shape):
    return lax.broadcasted_iota(jnp.int32, shape, 1)


def row_of(shape):
    return lax.broadcasted_iota(jnp.int32, shape, 0)


def row_next(a):
    return pltpu.roll(a, a.shape[0] - 1, 0)


def row_prev(a):
    return pltpu.roll(a, 1, 0)


def col_next(a):
    return pltpu.roll(a, a.shape[1] - 1, 1)


def col_prev(a):
    return pltpu.roll(a, 1, 1)


def pack_rims(fields):
    lane = lane_of(fields[0].shape)
    packed = pltpu.roll(fields[0], 8, 1)
    for index, field in enumerate(fields[1:], 1):
        moved = pltpu.roll(field, 16 * index + 8, 1)
        packed = jnp.where(lane >= 16 * index, moved, packed)
    return packed


def fold_rows(packed, width):
    high = width // 2
    folded = packed[0:high]
    lane = lane_of(folded.shape)
    for index in range(1, LANES // width):
        moved = pltpu.roll(packed[index * high : (index + 1) * high], index * width, 1)
        folded = jnp.where(lane >= index * width, moved, folded)
    return folded


def unfold_rows(folded, width):
    parts = [folded] + [pltpu.roll(folded, LANES - index * width, 1) for index in range(1, LANES // width)]
    return jnp.concatenate(parts, axis=0)


def ring(offset, size):
    return min(offset % size, -offset % size)


def far_first(pairs, distance):
    return sorted((p for p in pairs if any(p)), key=lambda p: (-distance(*p), p))


def kernel(
    n_grp,
    n_tile,
    base_velocity_in,
    viscosity_in,
    friction_in,
    friction_probe_in,
    pixel_los_in,
    pixel_weight_in,
    pixel_cell_in,
    pixel_count_in,
    panels,
    increment_out,
    probe_out,
    coef_out,
    base_velocity,
    viscosity,
    friction,
    friction_probe,
    pixel_los,
    pixel_weight,
    pixel_cell,
    pixel_count,
    ext,
    pack,
    side_r,
    side_l,
    slots_out,
    slots_in,
    coef,
    src,
    field,
    inc_stage,
    ext2,
    pack2,
    side2_r,
    side2_l,
    probe_stage,
    early_stage,
    early_in,
    late_stage,
    late_in,
    column,
    panel_buf,
    panel_ext,
    panel_rim,
    part_in,
    sum_in,
    halo_send,
    halo_recv,
    halo2_send,
    halo2_recv,
    rim_send,
    rim_recv,
    hand_send,
    hand_recv,
    local_sem,
    many_send,
    many_recv,
):
    g = lax.axis_index("grp")
    t = lax.axis_index("tile")
    up = lax.rem(g + n_grp - 1, n_grp)
    down = lax.rem(g + 1, n_grp)
    left = lax.rem(t + n_tile - 1, n_tile)
    right = lax.rem(t + 1, n_tile)

    y_size = 4
    x_size = n_grp // y_size
    z_size = n_tile // 4
    x, y_hi = lax.div(g, y_size), lax.rem(g, y_size)
    z, y_lo, core = lax.div(t, 4), lax.rem(lax.div(t, 2), 2), lax.rem(t, 2)
    y = 2 * y_hi + y_lo

    def tile_peer(dz, flip):
        lo = 1 - y_lo if flip >= 2 else y_lo
        side = 1 - core if flip % 2 else core
        return (g, 4 * lax.rem(z + dz, z_size) + 2 * lo + side)

    def grp_peer(dx, dy):
        return (y_size * lax.rem(x + dx, x_size) + lax.rem(y_hi + dy, y_size), t)

    def plane_peer(dx, dy):
        there = lax.rem(y + dy, 2 * y_size)
        return (y_size * lax.rem(x + dx, x_size) + lax.div(there, 2), 4 * z + 2 * lax.rem(there, 2) + core)

    def line_peer(dz, flip):
        return (g, 4 * lax.rem(z + dz, z_size) + 2 * y_lo + (1 - core if flip else core))

    tile_offsets = far_first(
        [(dz, flip) for dz in range(z_size) for flip in range(4)], lambda dz, flip: ring(dz, z_size) + (flip >= 2)
    )
    grp_offsets = far_first(
        [(dx, dy) for dx in range(x_size) for dy in range(y_size)],
        lambda dx, dy: ring(dx, x_size) + 2 * ring(dy, y_size),
    )
    plane_offsets = far_first(
        [(dx, dy) for dx in range(x_size) for dy in range(2 * y_size)],
        lambda dx, dy: ring(dx, x_size) + ring(dy, 2 * y_size),
    )
    line_offsets = far_first(
        [(dz, flip) for dz in range(z_size) for flip in range(2)], lambda dz, flip: ring(dz, z_size)
    )

    barrier = pltpu.get_barrier_semaphore()
    corners = [(a, b) for a in (up, down) for b in (left, right)]
    across = [plane_peer(*p) for p in plane_offsets if p[1] % 2]
    peers = corners + [(up, t), (down, t), (g, left), (g, right)]
    peers += [grp_peer(*p) for p in grp_offsets] + across + [tile_peer(*p) for p in tile_offsets if p != (0, 2)]
    for peer in peers:
        pl.semaphore_signal(barrier, inc=1, device_id=peer, device_id_type=MESH)

    loads = [
        pltpu.make_async_copy(a, b, local_sem.at[3 + index])
        for index, (a, b) in enumerate(
            [
                (base_velocity_in, base_velocity.at[:, pl.ds(HALO, 64)]),
                (viscosity_in, viscosity),
                (friction_in, friction),
                (friction_probe_in, friction_probe),
                (pixel_los_in.at[0, 0], pixel_los),
                (pixel_weight_in.at[0, 0], pixel_weight),
                (pixel_cell_in.at[0, 0], pixel_cell),
                (pixel_count_in.at[0, 0], pixel_count),
            ]
        )
    ]
    for load in loads:
        load.start()

    panel_copy = pltpu.make_async_copy(panels, panel_buf, local_sem.at[0])
    panel_copy.start()

    for load in loads[:4]:
        load.wait()
    bvx = base_velocity[0, HALO : HALO + 64]
    bvy = base_velocity[1, HALO : HALO + 64]
    fp = friction_probe[...]
    own = (viscosity[...], friction[...], -(fp * bvx), -(fp * bvy))
    for index in range(4):
        ext[index, HALO : HALO + 64, :] = own[index]
    packed = pack_rims(own)
    pack[0:8] = packed[0:8]
    pack[8:40] = fold_rows(packed, 64)
    pack[40:48] = packed[56:64]

    for load in loads[4:]:
        load.wait()
    odd = lax.rem(t, 2)
    lane1 = lane_of((1, LANES))
    for pair in range(n_tile // 2):
        lanes = slice(pair * LANES, (pair + 1) * LANES)
        count = jnp.where(lane1 < CAP, pixel_count[0, 2 * pair], pixel_count[0, 2 * pair + 1])
        live = lax.rem(lane1, CAP) < count
        block = jnp.concatenate(
            [
                pixel_los[:, lanes],
                jnp.where(live, pixel_weight[:, lanes], 0.0),
                pixel_cell[:, lanes].astype(F32),
            ],
            axis=0,
        )
        slots_out[pair] = jnp.where(odd == 1, pltpu.roll(block, CAP, 1), block)

    pl.semaphore_wait(barrier, len(peers))

    def remote(src_ref, dst_ref, send_sem, recv_sem, peer):
        return pltpu.make_async_remote_copy(
            src_ref=src_ref,
            dst_ref=dst_ref,
            send_sem=send_sem,
            recv_sem=recv_sem,
            device_id=peer,
            device_id_type=MESH,
        )

    def rim_copies(block, packed, from_right, from_left, send, recv):
        first, last = pl.ds(HALO, HALO), pl.ds(64, HALO)
        above, below = pl.ds(0, HALO), pl.ds(64 + HALO, HALO)
        high = packed.shape[0] - 16
        head, middle, tail = pl.ds(0, 8), pl.ds(8, high), pl.ds(8 + high, 8)
        moves = [
            (packed.at[head], from_right.at[tail], (up, left)),
            (packed.at[head], from_left.at[tail], (up, right)),
            (packed.at[tail], from_right.at[head], (down, left)),
            (packed.at[tail], from_left.at[head], (down, right)),
            (block.at[:, first], block.at[:, below], (up, t)),
            (block.at[:, last], block.at[:, above], (down, t)),
            (packed.at[middle], from_right.at[middle], (g, left)),
            (packed.at[middle], from_left.at[middle], (g, right)),
        ]
        return [remote(a, b, send.at[index], recv.at[index], peer) for index, (a, b, peer) in enumerate(moves)]

    def wait_bytes(ref, sem):
        pltpu.make_async_copy(ref, ref, sem).wait()

    copies = rim_copies(ext, pack, side_r, side_l, halo_send, halo_recv)
    for copy in copies:
        copy.start()
    first, last = pl.ds(HALO, HALO), pl.ds(64, HALO)
    above, below = pl.ds(0, HALO), pl.ds(64 + HALO, HALO)
    velocity_rims = [
        remote(base_velocity.at[:, first], base_velocity.at[:, below], rim_send.at[0], rim_recv.at[0], (up, t)),
        remote(base_velocity.at[:, last], base_velocity.at[:, above], rim_send.at[1], rim_recv.at[1], (down, t)),
    ]
    for copy in velocity_rims:
        copy.start()

    for dz, flip in tile_offsets:
        peer = tile_peer(dz, flip)
        remote(
            slots_out.at[lax.div(peer[1], 2)], slots_in.at[4 * dz + flip], many_send.at[0], many_recv.at[0], peer
        ).start()
    slots_in[0] = slots_out[lax.div(t, 2)]

    for copy in copies:
        copy.wait_recv()

    rows = 64 + 2 * HALO
    lane = lane_of((rows, LANES))
    row = row_of((rows, LANES))

    def merge(from_right, from_left):
        return jnp.where(lax.rem(lane_of(from_right.shape), 16) >= 8, from_right, from_left)

    def beside(merged, index):
        return pltpu.roll(merged, LANES - 16 * index - 8, 1)

    def widen(block, from_right, from_left):
        merged = merge(from_right[...], from_left[...])
        high = merged.shape[0] - 16
        middle = unfold_rows(merged[8 : 8 + high], 2 * high)
        merged = jnp.concatenate([merged[0:8], middle, merged[8 + high :]], axis=0)
        return [
            jnp.concatenate([block[index], beside(merged, index)], axis=1) for index in range(block.shape[0])
        ]

    v, fr, sx, sy = widen(ext, side_r, side_l)
    row_inside = ((row >= HALO) | (g > 0)) & ((row < HALO + 64) | (g < n_grp - 1))
    col_inside = ((lane < HALO) & (t < n_tile - 1)) | ((lane >= LANES - HALO) & (t > 0))
    inside = jnp.concatenate([row_inside, row_inside & col_inside], axis=1)
    v = jnp.where(inside, v, 0.0)
    pair_sum = v + row_next(v)
    east = 0.5 * pair_sum
    west = row_prev(east)
    north = 0.5 * (v + col_next(v))
    south = col_prev(north)
    node_pp = 0.0625 * (pair_sum + col_next(pair_sum))
    node_mp = row_prev(node_pp)
    node_pm = col_prev(node_pp)
    node_mm = col_prev(node_mp)
    diag_x = fr + 2.0 * (east + west) + (north + south)
    diag_y = fr + (east + west) + 2.0 * (north + south)
    inv_x = jnp.where(inside, RELAX / jnp.where(inside, diag_x, 1.0), 0.0)
    inv_y = jnp.where(inside, RELAX / jnp.where(inside, diag_y, 1.0), 0.0)
    for index, term in enumerate((east, west, north, south, node_pp, node_mp, node_pm, node_mm, inv_x, inv_y)):
        coef[index] = term
    src[0] = sx
    src[1] = sy

    def sweep(_, carry):
        cx, cy = field[0], field[1]
        ux, uy = row_next(cx), row_next(cy)
        dx, dy = row_prev(cx), row_prev(cy)
        e, w, n, s = coef[0], coef[1], coef[2], coef[3]
        pp, mp, pm, mm = coef[4], coef[5], coef[6], coef[7]
        ax = 2.0 * (e * ux + w * dx)
        ax += col_next(s * cx + (pm * uy - mm * dy))
        ax += col_prev(n * cx + (mp * dy - pp * uy))
        ay = e * uy + w * dy
        ay += col_next(2.0 * (s * cy) + (pm * ux - mm * dx))
        ay += col_prev(2.0 * (n * cy) + (mp * dx - pp * ux))
        field[0] = (1.0 - RELAX) * cx + coef[8] * (src[0] + ax)
        field[1] = (1.0 - RELAX) * cy + coef[9] * (src[1] + ay)
        return carry

    def relax():
        field[0] = coef[8] * src[0]
        field[1] = coef[9] * src[1]
        lax.fori_loop(1, SWEEPS, sweep, 0)

    def probe_of(at):
        return -(base_velocity[0, at] * field[0, at, :LANES] + base_velocity[1, at] * field[1, at, :LANES])

    own_rows = slice(HALO, HALO + 64)
    relax()
    inc_x, inc_y = field[0, own_rows, :LANES], field[1, own_rows, :LANES]
    inc_stage[0] = inc_x
    inc_stage[1] = inc_y
    increment_copy = pltpu.make_async_copy(inc_stage, increment_out, local_sem.at[1])
    increment_copy.start()

    wait_bytes(slots_in.at[pl.ds(0, n_tile - 1)], many_recv.at[0])

    def halves(a):
        high = a.astype(BF16)
        return high, (a - high.astype(F32)).astype(BF16)

    xh, xl = halves(inc_x)
    yh, yl = halves(inc_y)
    stacked = jnp.concatenate([xh, yh, xl, yl], axis=0)
    chunk = 2 * LANES
    total = jnp.zeros((256, LANES), F32)
    low_half = lane_of((4, LANES)) < CAP
    for index in range(n_tile * CAP // chunk):
        first = jnp.where(low_half, slots_in[4 * index], slots_in[4 * index + 1])
        second = jnp.where(low_half, slots_in[4 * index + 2], slots_in[4 * index + 3])
        lists = jnp.concatenate([first, second], axis=1)
        los_x, los_y, weight = lists[0:1], lists[1:2], lists[2:3]
        cell = lists[3:4].astype(jnp.int32)
        at_col = row_of((LANES, chunk)) == (cell & (LANES - 1))
        at_row = row_of((64, chunk)) == (cell >> 7)
        col_hot = jnp.where(at_col, 1.0, 0.0).astype(BF16)
        found = jnp.dot(stacked, col_hot, preferred_element_type=F32)
        got_x = jnp.sum(jnp.where(at_row, found[0:64] + found[128:192], 0.0), axis=0, keepdims=True)
        got_y = jnp.sum(jnp.where(at_row, found[64:128] + found[192:256], 0.0), axis=0, keepdims=True)
        amount = weight * (los_x * got_x + los_y * got_y)
        scaled = []
        for value in (amount * los_x, amount * los_y):
            high = value.astype(BF16).astype(F32)
            scaled.append((high, value - high))
        hot = [
            jnp.where(at_row, jnp.broadcast_to(part, (64, chunk)), 0.0)
            for part in (scaled[0][0], scaled[1][0], scaled[0][1], scaled[1][1])
        ]
        hot = jnp.concatenate(hot, axis=0).astype(BF16)
        total += lax.dot_general(hot, col_hot, (((1,), (1,)), ((), ())), preferred_element_type=F32)
    adjoint = (total[0:64] + total[128:192], total[64:128] + total[192:256])

    for index in range(2):
        ext2[index, HALO : HALO + 64, :] = adjoint[index]
    packed2 = pack_rims(adjoint)
    pack2[0:8] = packed2[0:8]
    pack2[8:24] = fold_rows(packed2, 32)
    pack2[24:32] = packed2[56:64]
    copies2 = rim_copies(ext2, pack2, side2_r, side2_l, halo2_send, halo2_recv)
    for copy in copies2[6:] + copies2[:6]:
        copy.start()

    for index in range(2):
        src[index] = jnp.zeros((rows, 2 * LANES), F32)
        src[index, own_rows, :LANES] = adjoint[index]
    relax()
    for copy in velocity_rims:
        copy.wait_recv()
    everything = slice(0, rows)
    part = probe_of(everything).astype(BF16)
    early_stage[...] = part
    early_in[g] = part
    opposite = grp_peer(0, y_size // 2)
    handed_on = [(dx, 0) for dx in range(1, x_size)]
    direct = [offset for offset in grp_offsets if offset[1] != y_size // 2]
    remote(early_stage, early_in.at[g], hand_send.at[0], hand_recv.at[0], opposite).start()
    for offset in direct:
        remote(early_stage, early_in.at[g], many_send.at[1], many_recv.at[1], grp_peer(*offset)).start()

    panel_copy.wait()
    panel_ext[0:HALO] = jnp.zeros((HALO, LANES), F32)
    panel_ext[HALO + 64 * n_grp :] = jnp.zeros((HALO, LANES), F32)
    fold_lane = lane_of((16, LANES))

    def fold_late(block, start):
        folded = jnp.zeros((16, LANES), F32)
        for j in range(rows // 16):
            moved = pltpu.roll(block[start + 16 * j : start + 16 * j + 16, :], 16 * j + 8, 1)
            here = (fold_lane >= 16 * j) & (fold_lane < 16 * j + 16)
            folded = jnp.where(here, moved, folded)
        return folded

    def fold_panel(k, carry):
        panel_ext[HALO : HALO + 64 * n_grp] = panel_buf[k].astype(F32)
        for block in range(n_grp):
            panel_rim[k, block] = fold_late(panel_ext, 64 * block)
        return carry

    lax.fori_loop(0, 8, fold_panel, 0)

    for copy in copies2[6:]:
        copy.wait_recv()
    middle = unfold_rows(merge(side2_r[8:24], side2_l[8:24]), 32)
    for index in range(2):
        src[index, own_rows, LANES:] = beside(middle, index)
    relax()
    late = fold_late(probe_of(everything), 0).astype(BF16)
    late_stage[...] = late
    late_in[g] = late
    for offset in grp_offsets:
        remote(late_stage, late_in.at[g], many_send.at[2], many_recv.at[2], grp_peer(*offset)).start()

    wait_bytes(early_in.at[0], hand_recv.at[0])
    for offset in handed_on:
        remote(
            early_in.at[opposite[0]], early_in.at[opposite[0]], hand_send.at[1], hand_recv.at[1], grp_peer(*offset)
        ).start()

    for copy in copies2[:6]:
        copy.wait_recv()
    for at, edge in ((slice(0, 8), slice(0, 8)), (slice(64 + HALO, rows), slice(24, 32))):
        merged = merge(side2_r[edge], side2_l[edge])
        for index in range(2):
            src[index, at, :LANES] = ext2[index, at]
            src[index, at, LANES:] = beside(merged, index)
    relax()
    probe_stage[...] = probe_of(own_rows)
    probe_copy = pltpu.make_async_copy(probe_stage, probe_out, local_sem.at[2])
    probe_copy.start()

    wait_bytes(early_in.at[pl.ds(0, len(direct))], many_recv.at[1])
    if handed_on:
        wait_bytes(early_in.at[pl.ds(0, len(handed_on))], hand_recv.at[1])
    column[...] = jnp.zeros_like(column)
    part_lane = lane_of((rows, LANES))
    is_middle = (part_lane >= HALO) & (part_lane < LANES - HALO)
    for block in range(n_grp):
        at = slice(64 * block, 64 * block + rows)
        column[at] += jnp.where(is_middle, early_in[block].astype(F32), 0.0)

    def project(block, sums):
        start = pl.multiple_of(block * 64, 64)
        values = column[pl.ds(start + HALO, 64), :]
        return tuple(
            total + jnp.sum((panel_buf[k, pl.ds(start, 64), :].astype(F32) * values).reshape(8, 8, LANES), axis=0)
            for k, total in enumerate(sums)
        )

    sums = lax.fori_loop(0, n_grp, project, tuple(jnp.zeros((8, LANES), F32) for _ in range(8)))
    wait_bytes(late_in.at[pl.ds(0, n_grp - 1)], many_recv.at[2])
    sums = list(sums)
    for block in range(n_grp):
        late = late_in[block].astype(F32)
        for k in range(8):
            product = panel_rim[k, block] * late
            sums[k] = sums[k] + product[0:8] + product[8:16]
    partial = jnp.concatenate([jnp.sum(s, axis=0, keepdims=True) for s in sums], axis=0)
    partial = jnp.sum(partial, axis=1, keepdims=True)
    mine = lane_of((8, LANES)) == 8 * g + row_of((8, LANES))
    placed = jnp.sum(jnp.where(mine, jnp.broadcast_to(partial, (8, LANES)), 0.0), axis=0, keepdims=True)

    def sum_over(value, landing, offsets, peer, index):
        landing[0] = value
        for slot, offset in enumerate(offsets, 1):
            remote(
                landing.at[0], landing.at[slot], many_send.at[index], many_recv.at[index], peer(*offset)
            ).start()
        wait_bytes(landing.at[pl.ds(1, len(offsets))], many_recv.at[index])
        return jnp.sum(landing[...], axis=0)

    plane_sum = sum_over(placed, part_in, plane_offsets, plane_peer, 3)
    coef_out[...] = sum_over(plane_sum, sum_in, line_offsets, line_peer, 4)

    for copy in copies + velocity_rims + copies2:
        copy.wait_send()
    wait_bytes(slots_in.at[pl.ds(0, n_tile - 1)], many_send.at[0])
    wait_bytes(early_in.at[pl.ds(0, len(direct))], many_send.at[1])
    wait_bytes(early_in.at[0], hand_send.at[0])
    if handed_on:
        wait_bytes(early_in.at[pl.ds(0, len(handed_on))], hand_send.at[1])
    wait_bytes(late_in.at[pl.ds(0, n_grp - 1)], many_send.at[2])
    wait_bytes(part_in.at[pl.ds(1, len(plane_offsets))], many_send.at[3])
    wait_bytes(sum_in.at[pl.ds(1, len(line_offsets))], many_send.at[4])
    increment_copy.wait()
    probe_copy.wait()


def on_device(n_grp, n_tile, base_velocity, viscosity, friction, friction_probe, pixel_los, pixel_weight, pixel_cell, pixel_count, panels):
    slots = pixel_los.shape[-1]
    panel_rows = panels.shape[1]
    vmem = pl.BlockSpec(memory_space=pltpu.VMEM)
    hbm = pl.BlockSpec(memory_space=pltpu.HBM)
    wide = 64 + 2 * HALO
    increment, probe, coefficients = pl.pallas_call(
        functools.partial(kernel, n_grp, n_tile),
        out_shape=(
            jax.ShapeDtypeStruct((2, 64, LANES), F32),
            jax.ShapeDtypeStruct((64, LANES), F32),
            jax.ShapeDtypeStruct((1, LANES), F32),
        ),
        in_specs=[hbm] * 9,
        out_specs=(hbm, hbm, vmem),
        scratch_shapes=[
            pltpu.VMEM((2, wide, LANES), F32),
            pltpu.VMEM((64, LANES), F32),
            pltpu.VMEM((64, LANES), F32),
            pltpu.VMEM((64, LANES), F32),
            pltpu.VMEM((2, slots), F32),
            pltpu.VMEM((1, slots), F32),
            pltpu.VMEM((1, slots), jnp.int32),
            pltpu.SMEM((1, n_tile), jnp.int32),
            pltpu.VMEM((4, wide, LANES), F32),
            pltpu.VMEM((48, LANES), F32),
            pltpu.VMEM((48, LANES), F32),
            pltpu.VMEM((48, LANES), F32),
            pltpu.VMEM((n_tile // 2, 4, LANES), F32),
            pltpu.VMEM((n_tile, 4, LANES), F32),
            pltpu.VMEM((10, wide, 2 * LANES), F32),
            pltpu.VMEM((2, wide, 2 * LANES), F32),
            pltpu.VMEM((2, wide, 2 * LANES), F32),
            pltpu.VMEM((2, 64, LANES), F32),
            pltpu.VMEM((2, wide, LANES), F32),
            pltpu.VMEM((32, LANES), F32),
            pltpu.VMEM((32, LANES), F32),
            pltpu.VMEM((32, LANES), F32),
            pltpu.VMEM((64, LANES), F32),
            pltpu.VMEM((wide, LANES), BF16),
            pltpu.VMEM((n_grp, wide, LANES), BF16),
            pltpu.VMEM((16, LANES), BF16),
            pltpu.VMEM((n_grp, 16, LANES), BF16),
            pltpu.VMEM((panel_rows + 2 * HALO, LANES), F32),
            pltpu.VMEM((8, panel_rows, LANES), BF16),
            pltpu.VMEM((panel_rows + 2 * HALO, LANES), F32),
            pltpu.VMEM((8, n_grp, 16, LANES), F32),
            pltpu.VMEM((2 * n_grp, 1, LANES), F32),
            pltpu.VMEM((n_tile // 2, 1, LANES), F32),
            pltpu.SemaphoreType.DMA((8,)),
            pltpu.SemaphoreType.DMA((8,)),
            pltpu.SemaphoreType.DMA((8,)),
            pltpu.SemaphoreType.DMA((8,)),
            pltpu.SemaphoreType.DMA((2,)),
            pltpu.SemaphoreType.DMA((2,)),
            pltpu.SemaphoreType.DMA((2,)),
            pltpu.SemaphoreType.DMA((2,)),
            pltpu.SemaphoreType.DMA((11,)),
            pltpu.SemaphoreType.DMA((5,)),
            pltpu.SemaphoreType.DMA((5,)),
        ],
        compiler_params=pltpu.CompilerParams(
            collective_id=0, has_side_effects=True, vmem_limit_bytes=24 * 1024 * 1024
        ),
    )(
        *(
            pltpu.with_memory_space_constraint(a, pltpu.HBM)
            for a in (
                base_velocity,
                viscosity,
                friction,
                friction_probe,
                pixel_los,
                pixel_weight,
                pixel_cell,
                pixel_count,
                panels,
            )
        )
    )
    return increment, probe, coefficients.reshape(LANES)[: 8 * n_grp]


def solution(mesh):
    in_specs = (
        P(None, "grp", "tile"),
        P("grp", "tile"),
        P("grp", "tile"),
        P("grp", "tile"),
        P("grp", "tile", None, None),
        P("grp", "tile", None, None),
        P("grp", "tile", None, None),
        P("grp", "tile", None, None),
        P("grp", None, "tile"),
    )
    out_specs = (P(None, "grp", "tile"), P("grp", "tile"), P())
    body = functools.partial(on_device, mesh.shape["grp"], mesh.shape["tile"])
    return jax.shard_map(body, mesh=mesh, in_specs=in_specs, out_specs=out_specs, check_vma=False)
```

```python
import functools

import jax
import jax.numpy as jnp
from jax import lax
from jax.experimental import pallas as pl
from jax.experimental.pallas import tpu as pltpu
from jax.sharding import PartitionSpec as P

SWEEPS = 8
RELAX = 0.8
HALO = 8
CAP = 64
LANES = 128
MESH = pl.DeviceIdType.MESH
F32 = jnp.float32
BF16 = jnp.bfloat16


def lane_of(shape):
    return lax.broadcasted_iota(jnp.int32, shape, 1)


def row_of(shape):
    return lax.broadcasted_iota(jnp.int32, shape, 0)


def row_next(a):
    return pltpu.roll(a, a.shape[0] - 1, 0)


def row_prev(a):
    return pltpu.roll(a, 1, 0)


def col_next(a):
    return pltpu.roll(a, a.shape[1] - 1, 1)


def col_prev(a):
    return pltpu.roll(a, 1, 1)


def pack_rims(fields):
    lane = lane_of(fields[0].shape)
    packed = pltpu.roll(fields[0], 8, 1)
    for index, field in enumerate(fields[1:], 1):
        moved = pltpu.roll(field, 16 * index + 8, 1)
        packed = jnp.where(lane >= 16 * index, moved, packed)
    return packed


def fold_rows(packed, width):
    high = width // 2
    folded = packed[0:high]
    lane = lane_of(folded.shape)
    for index in range(1, LANES // width):
        moved = pltpu.roll(packed[index * high : (index + 1) * high], index * width, 1)
        folded = jnp.where(lane >= index * width, moved, folded)
    return folded


def unfold_rows(folded, width):
    parts = [folded] + [pltpu.roll(folded, LANES - index * width, 1) for index in range(1, LANES // width)]
    return jnp.concatenate(parts, axis=0)


def ring(offset, size):
    return min(offset % size, -offset % size)


def far_first(pairs, distance):
    return sorted((p for p in pairs if any(p)), key=lambda p: (-distance(*p), p))


def kernel(
    n_grp,
    n_tile,
    base_velocity_in,
    viscosity_in,
    friction_in,
    friction_probe_in,
    pixel_los_in,
    pixel_weight_in,
    pixel_cell_in,
    pixel_count_in,
    panels,
    increment_out,
    probe_out,
    coef_out,
    base_velocity,
    viscosity,
    friction,
    friction_probe,
    pixel_los,
    pixel_weight,
    pixel_cell,
    pixel_count,
    ext,
    pack,
    side_r,
    side_l,
    slots_out,
    slots_in,
    coef,
    src,
    field,
    other,
    ext2,
    pack2,
    side2_r,
    side2_l,
    early_stage,
    early_in,
    late_stage,
    late_in,
    column,
    panel_buf,
    panel_ext,
    panel_rim,
    part_in,
    sum_in,
    halo_send,
    halo_recv,
    halo2_send,
    halo2_recv,
    rim_send,
    rim_recv,
    hand_send,
    hand_recv,
    local_sem,
    many_send,
    many_recv,
):
    g = lax.axis_index("grp")
    t = lax.axis_index("tile")
    up = lax.rem(g + n_grp - 1, n_grp)
    down = lax.rem(g + 1, n_grp)
    left = lax.rem(t + n_tile - 1, n_tile)
    right = lax.rem(t + 1, n_tile)

    y_size = 4
    x_size = n_grp // y_size
    z_size = n_tile // 4
    x, y_hi = lax.div(g, y_size), lax.rem(g, y_size)
    z, y_lo, core = lax.div(t, 4), lax.rem(lax.div(t, 2), 2), lax.rem(t, 2)
    y = 2 * y_hi + y_lo

    def tile_peer(dz, flip):
        lo = 1 - y_lo if flip >= 2 else y_lo
        side = 1 - core if flip % 2 else core
        return (g, 4 * lax.rem(z + dz, z_size) + 2 * lo + side)

    def grp_peer(dx, dy):
        return (y_size * lax.rem(x + dx, x_size) + lax.rem(y_hi + dy, y_size), t)

    def plane_peer(dx, dy):
        there = lax.rem(y + dy, 2 * y_size)
        return (y_size * lax.rem(x + dx, x_size) + lax.div(there, 2), 4 * z + 2 * lax.rem(there, 2) + core)

    def line_peer(dz, flip):
        return (g, 4 * lax.rem(z + dz, z_size) + 2 * y_lo + (1 - core if flip else core))

    tile_offsets = far_first(
        [(dz, flip) for dz in range(z_size) for flip in range(4)], lambda dz, flip: ring(dz, z_size) + (flip >= 2)
    )
    grp_offsets = far_first(
        [(dx, dy) for dx in range(x_size) for dy in range(y_size)],
        lambda dx, dy: ring(dx, x_size) + 2 * ring(dy, y_size),
    )
    plane_offsets = far_first(
        [(dx, dy) for dx in range(x_size) for dy in range(2 * y_size)],
        lambda dx, dy: ring(dx, x_size) + ring(dy, 2 * y_size),
    )
    line_offsets = far_first(
        [(dz, flip) for dz in range(z_size) for flip in range(2)], lambda dz, flip: ring(dz, z_size)
    )

    barrier = pltpu.get_barrier_semaphore()
    corners = [(a, b) for a in (up, down) for b in (left, right)]
    across = [plane_peer(*p) for p in plane_offsets if p[1] % 2]
    peers = corners + [(up, t), (down, t), (g, left), (g, right)]
    peers += [grp_peer(*p) for p in grp_offsets] + across + [tile_peer(*p) for p in tile_offsets if p != (0, 2)]
    for peer in peers:
        pl.semaphore_signal(barrier, inc=1, device_id=peer, device_id_type=MESH)

    loads = [
        pltpu.make_async_copy(a, b, local_sem.at[1 + index])
        for index, (a, b) in enumerate(
            [
                (base_velocity_in, base_velocity.at[:, pl.ds(HALO, 64)]),
                (viscosity_in, viscosity),
                (friction_in, friction),
                (friction_probe_in, friction_probe),
                (pixel_los_in.at[0, 0], pixel_los),
                (pixel_weight_in.at[0, 0], pixel_weight),
                (pixel_cell_in.at[0, 0], pixel_cell),
                (pixel_count_in.at[0, 0], pixel_count),
            ]
        )
    ]
    for load in loads:
        load.start()

    panel_copy = pltpu.make_async_copy(panels, panel_buf, local_sem.at[0])
    panel_copy.start()

    for load in loads[:4]:
        load.wait()
    bvx = base_velocity[0, HALO : HALO + 64]
    bvy = base_velocity[1, HALO : HALO + 64]
    fp = friction_probe[...]
    own = (viscosity[...], friction[...], -(fp * bvx), -(fp * bvy))
    for index in range(4):
        ext[index, HALO : HALO + 64, :] = own[index]
    packed = pack_rims(own)
    pack[0:8] = packed[0:8]
    pack[8:40] = fold_rows(packed, 64)
    pack[40:48] = packed[56:64]

    for load in loads[4:]:
        load.wait()
    odd = lax.rem(t, 2)
    lane1 = lane_of((1, LANES))
    for pair in range(n_tile // 2):
        lanes = slice(pair * LANES, (pair + 1) * LANES)
        count = jnp.where(lane1 < CAP, pixel_count[0, 2 * pair], pixel_count[0, 2 * pair + 1])
        live = lax.rem(lane1, CAP) < count
        block = jnp.concatenate(
            [
                pixel_los[:, lanes],
                jnp.where(live, pixel_weight[:, lanes], 0.0),
                pixel_cell[:, lanes].astype(F32),
            ],
            axis=0,
        )
        slots_out[pair] = jnp.where(odd == 1, pltpu.roll(block, CAP, 1), block)

    pl.semaphore_wait(barrier, len(peers))

    def remote(src_ref, dst_ref, send_sem, recv_sem, peer):
        return pltpu.make_async_remote_copy(
            src_ref=src_ref,
            dst_ref=dst_ref,
            send_sem=send_sem,
            recv_sem=recv_sem,
            device_id=peer,
            device_id_type=MESH,
        )

    def rim_copies(block, packed, from_right, from_left, send, recv):
        first, last = pl.ds(HALO, HALO), pl.ds(64, HALO)
        above, below = pl.ds(0, HALO), pl.ds(64 + HALO, HALO)
        high = packed.shape[0] - 16
        head, middle, tail = pl.ds(0, 8), pl.ds(8, high), pl.ds(8 + high, 8)
        moves = [
            (packed.at[head], from_right.at[tail], (up, left)),
            (packed.at[head], from_left.at[tail], (up, right)),
            (packed.at[tail], from_right.at[head], (down, left)),
            (packed.at[tail], from_left.at[head], (down, right)),
            (block.at[:, first], block.at[:, below], (up, t)),
            (block.at[:, last], block.at[:, above], (down, t)),
            (packed.at[middle], from_right.at[middle], (g, left)),
            (packed.at[middle], from_left.at[middle], (g, right)),
        ]
        return [remote(a, b, send.at[index], recv.at[index], peer) for index, (a, b, peer) in enumerate(moves)]

    def wait_bytes(ref, sem):
        pltpu.make_async_copy(ref, ref, sem).wait()

    copies = rim_copies(ext, pack, side_r, side_l, halo_send, halo_recv)
    for copy in copies:
        copy.start()
    first, last = pl.ds(HALO, HALO), pl.ds(64, HALO)
    above, below = pl.ds(0, HALO), pl.ds(64 + HALO, HALO)
    velocity_rims = [
        remote(base_velocity.at[:, first], base_velocity.at[:, below], rim_send.at[0], rim_recv.at[0], (up, t)),
        remote(base_velocity.at[:, last], base_velocity.at[:, above], rim_send.at[1], rim_recv.at[1], (down, t)),
    ]
    for copy in velocity_rims:
        copy.start()

    for dz, flip in tile_offsets:
        peer = tile_peer(dz, flip)
        remote(
            slots_out.at[lax.div(peer[1], 2)], slots_in.at[4 * dz + flip], many_send.at[0], many_recv.at[0], peer
        ).start()
    slots_in[0] = slots_out[lax.div(t, 2)]

    for copy in copies:
        copy.wait_recv()

    rows = 64 + 2 * HALO
    lane = lane_of((rows, LANES))
    row = row_of((rows, LANES))

    def merge(from_right, from_left):
        return jnp.where(lax.rem(lane_of(from_right.shape), 16) >= 8, from_right, from_left)

    def beside(merged, index):
        return pltpu.roll(merged, LANES - 16 * index - 8, 1)

    def widen(block, from_right, from_left):
        merged = merge(from_right[...], from_left[...])
        high = merged.shape[0] - 16
        middle = unfold_rows(merged[8 : 8 + high], 2 * high)
        merged = jnp.concatenate([merged[0:8], middle, merged[8 + high :]], axis=0)
        return [
            jnp.concatenate([block[index], beside(merged, index)], axis=1) for index in range(block.shape[0])
        ]

    v, fr, sx, sy = widen(ext, side_r, side_l)
    row_inside = ((row >= HALO) | (g > 0)) & ((row < HALO + 64) | (g < n_grp - 1))
    col_inside = ((lane < HALO) & (t < n_tile - 1)) | ((lane >= LANES - HALO) & (t > 0))
    inside = jnp.concatenate([row_inside, row_inside & col_inside], axis=1)
    v = jnp.where(inside, v, 0.0)
    pair_sum = v + row_next(v)
    east = 0.5 * pair_sum
    west = row_prev(east)
    north = 0.5 * (v + col_next(v))
    south = col_prev(north)
    node_pp = 0.0625 * (pair_sum + col_next(pair_sum))
    node_mp = row_prev(node_pp)
    node_pm = col_prev(node_pp)
    node_mm = col_prev(node_mp)
    diag_x = fr + 2.0 * (east + west) + (north + south)
    diag_y = fr + (east + west) + 2.0 * (north + south)
    inv_x = jnp.where(inside, RELAX / jnp.where(inside, diag_x, 1.0), 0.0)
    inv_y = jnp.where(inside, RELAX / jnp.where(inside, diag_y, 1.0), 0.0)
    for index, term in enumerate((east, west, north, south, node_pp, node_mp, node_pm, node_mm, inv_x, inv_y)):
        coef[index, 0] = term[:, :LANES]
        coef[index, 1] = term[:, LANES:]
    for index, term in enumerate((sx, sy)):
        src[index, 0] = term[:, :LANES]
        src[index, 1] = term[:, LANES:]
    for buffer in (field, other):
        buffer[:, :, 0:HALO] = jnp.zeros((2, 2, HALO, LANES), F32)
        buffer[:, :, HALO + rows :] = jnp.zeros((2, 2, HALO, LANES), F32)
    tile_lane = lane_of((8, LANES))
    at_last, at_first = tile_lane == LANES - 1, tile_lane == 0

    def pair_next(pair):
        own, rim = (pltpu.roll(a, LANES - 1, 1) for a in pair)
        return jnp.where(at_last, rim, own), jnp.where(at_last, own, rim)

    def pair_prev(pair):
        own, rim = (pltpu.roll(a, 1, 1) for a in pair)
        return jnp.where(at_first, rim, own), jnp.where(at_first, own, rim)

    def sweep(now, later):
        for tile in range(rows // 8):
            at = slice(8 * tile, 8 * tile + 8)
            inner = slice(8 * tile + HALO, 8 * tile + HALO + 8)
            after = slice(8 * tile + HALO + 1, 8 * tile + HALO + 9)
            before = slice(8 * tile + HALO - 1, 8 * tile + HALO + 7)
            axial, forward, backward, centre = ([], []), ([], []), ([], []), ([], [])
            for part in range(2):
                e, w, n, s, pp, mp, pm, mm = (coef[index, part, at] for index in range(8))
                cx, cy = now[0, part, inner], now[1, part, inner]
                ux, uy = now[0, part, after], now[1, part, after]
                dx, dy = now[0, part, before], now[1, part, before]
                ax = e * ux + w * dx
                cy2 = cy + cy
                axial[0].append(ax + ax)
                axial[1].append(e * uy + w * dy)
                forward[0].append(s * cx + (pm * uy - mm * dy))
                forward[1].append(s * cy2 + (pm * ux - mm * dx))
                backward[0].append(n * cx + (mp * dy - pp * uy))
                backward[1].append(n * cy2 + (mp * dx - pp * ux))
                centre[0].append(cx)
                centre[1].append(cy)
            for index in range(2):
                ahead, behind = pair_next(forward[index]), pair_prev(backward[index])
                for part in range(2):
                    total = src[index, part, at] + axial[index][part] + (ahead[part] + behind[part])
                    later[index, part, inner] = (1.0 - RELAX) * centre[index][part] + (
                        coef[8 + index, part, at] * total
                    )

    def two_sweeps(_, carry):
        sweep(other, field)
        sweep(field, other)
        return carry

    def relax():
        for index in range(2):
            other[index, :, HALO : HALO + rows] = coef[8 + index] * src[index]
        lax.fori_loop(0, (SWEEPS - 2) // 2, two_sweeps, 0)
        sweep(other, field)

    def solved(index, at):
        return field[index, 0, at.start + HALO : at.stop + HALO]

    def probe_of(at):
        return -(base_velocity[0, at] * solved(0, at) + base_velocity[1, at] * solved(1, at))

    own_rows = slice(HALO, HALO + 64)
    relax()
    inc_x, inc_y = solved(0, own_rows), solved(1, own_rows)
    increment_out[0] = inc_x
    increment_out[1] = inc_y

    wait_bytes(slots_in.at[pl.ds(0, n_tile - 1)], many_recv.at[0])

    def halves(a):
        high = a.astype(BF16)
        return high, (a - high.astype(F32)).astype(BF16)

    xh, xl = halves(inc_x)
    yh, yl = halves(inc_y)
    stacked = jnp.concatenate([xh, yh, xl, yl], axis=0)
    chunk = 2 * LANES
    total = jnp.zeros((256, LANES), F32)
    low_half = lane_of((4, LANES)) < CAP
    for index in range(n_tile * CAP // chunk):
        first = jnp.where(low_half, slots_in[4 * index], slots_in[4 * index + 1])
        second = jnp.where(low_half, slots_in[4 * index + 2], slots_in[4 * index + 3])
        lists = jnp.concatenate([first, second], axis=1)
        los_x, los_y, weight = lists[0:1], lists[1:2], lists[2:3]
        cell = lists[3:4].astype(jnp.int32)
        at_col = row_of((LANES, chunk)) == (cell & (LANES - 1))
        at_row = row_of((64, chunk)) == (cell >> 7)
        col_hot = jnp.where(at_col, 1.0, 0.0).astype(BF16)
        found = jnp.dot(stacked, col_hot, preferred_element_type=F32)
        got_x = jnp.sum(jnp.where(at_row, found[0:64] + found[128:192], 0.0), axis=0, keepdims=True)
        got_y = jnp.sum(jnp.where(at_row, found[64:128] + found[192:256], 0.0), axis=0, keepdims=True)
        amount = weight * (los_x * got_x + los_y * got_y)
        scaled = []
        for value in (amount * los_x, amount * los_y):
            high = value.astype(BF16).astype(F32)
            scaled.append((high, value - high))
        hot = [
            jnp.where(at_row, jnp.broadcast_to(part, (64, chunk)), 0.0)
            for part in (scaled[0][0], scaled[1][0], scaled[0][1], scaled[1][1])
        ]
        hot = jnp.concatenate(hot, axis=0).astype(BF16)
        total += lax.dot_general(hot, col_hot, (((1,), (1,)), ((), ())), preferred_element_type=F32)
    adjoint = (total[0:64] + total[128:192], total[64:128] + total[192:256])

    for index in range(2):
        ext2[index, HALO : HALO + 64, :] = adjoint[index]
    packed2 = pack_rims(adjoint)
    pack2[0:8] = packed2[0:8]
    pack2[8:24] = fold_rows(packed2, 32)
    pack2[24:32] = packed2[56:64]
    copies2 = rim_copies(ext2, pack2, side2_r, side2_l, halo2_send, halo2_recv)
    for copy in copies2[6:] + copies2[:6]:
        copy.start()

    for index in range(2):
        src[index] = jnp.zeros((2, rows, LANES), F32)
        src[index, 0, own_rows] = adjoint[index]
    relax()
    for copy in velocity_rims:
        copy.wait_recv()
    everything = slice(0, rows)
    part = probe_of(everything).astype(BF16)
    early_stage[...] = part
    early_in[g] = part
    opposite = grp_peer(0, y_size // 2)
    handed_on = [(dx, 0) for dx in range(1, x_size)]
    direct = [offset for offset in grp_offsets if offset[1] != y_size // 2]
    remote(early_stage, early_in.at[g], hand_send.at[0], hand_recv.at[0], opposite).start()
    for offset in direct:
        remote(early_stage, early_in.at[g], many_send.at[1], many_recv.at[1], grp_peer(*offset)).start()

    panel_copy.wait()
    panel_ext[0:HALO] = jnp.zeros((HALO, LANES), F32)
    panel_ext[HALO + 64 * n_grp :] = jnp.zeros((HALO, LANES), F32)
    fold_lane = lane_of((16, LANES))

    def fold_late(block, start):
        folded = jnp.zeros((16, LANES), F32)
        for j in range(rows // 16):
            moved = pltpu.roll(block[start + 16 * j : start + 16 * j + 16, :], 16 * j + 8, 1)
            here = (fold_lane >= 16 * j) & (fold_lane < 16 * j + 16)
            folded = jnp.where(here, moved, folded)
        return folded

    def fold_panel(k, carry):
        panel_ext[HALO : HALO + 64 * n_grp] = panel_buf[k].astype(F32)
        for block in range(n_grp):
            panel_rim[k, block] = fold_late(panel_ext, 64 * block)
        return carry

    lax.fori_loop(0, 8, fold_panel, 0)

    for copy in copies2[6:]:
        copy.wait_recv()
    middle = unfold_rows(merge(side2_r[8:24], side2_l[8:24]), 32)
    for index in range(2):
        src[index, 1, own_rows] = beside(middle, index)
    relax()
    late = fold_late(probe_of(everything), 0).astype(BF16)
    late_stage[...] = late
    late_in[g] = late
    for offset in grp_offsets:
        remote(late_stage, late_in.at[g], many_send.at[2], many_recv.at[2], grp_peer(*offset)).start()

    wait_bytes(early_in.at[0], hand_recv.at[0])
    for offset in handed_on:
        remote(
            early_in.at[opposite[0]], early_in.at[opposite[0]], hand_send.at[1], hand_recv.at[1], grp_peer(*offset)
        ).start()

    for copy in copies2[:6]:
        copy.wait_recv()
    for at, edge in ((slice(0, 8), slice(0, 8)), (slice(64 + HALO, rows), slice(24, 32))):
        merged = merge(side2_r[edge], side2_l[edge])
        for index in range(2):
            src[index, 0, at] = ext2[index, at]
            src[index, 1, at] = beside(merged, index)
    relax()
    probe_out[...] = probe_of(own_rows)

    wait_bytes(early_in.at[pl.ds(0, len(direct))], many_recv.at[1])
    if handed_on:
        wait_bytes(early_in.at[pl.ds(0, len(handed_on))], hand_recv.at[1])
    column[...] = jnp.zeros_like(column)
    part_lane = lane_of((rows, LANES))
    is_middle = (part_lane >= HALO) & (part_lane < LANES - HALO)
    for block in range(n_grp):
        at = slice(64 * block, 64 * block + rows)
        column[at] += jnp.where(is_middle, early_in[block].astype(F32), 0.0)

    def project(block, sums):
        start = pl.multiple_of(block * 64, 64)
        values = column[pl.ds(start + HALO, 64), :]
        return tuple(
            total + jnp.sum((panel_buf[k, pl.ds(start, 64), :].astype(F32) * values).reshape(8, 8, LANES), axis=0)
            for k, total in enumerate(sums)
        )

    sums = lax.fori_loop(0, n_grp, project, tuple(jnp.zeros((8, LANES), F32) for _ in range(8)))
    wait_bytes(late_in.at[pl.ds(0, n_grp - 1)], many_recv.at[2])
    sums = list(sums)
    for block in range(n_grp):
        late = late_in[block].astype(F32)
        for k in range(8):
            product = panel_rim[k, block] * late
            sums[k] = sums[k] + product[0:8] + product[8:16]
    partial = jnp.concatenate([jnp.sum(s, axis=0, keepdims=True) for s in sums], axis=0)
    partial = jnp.sum(partial, axis=1, keepdims=True)
    mine = lane_of((8, LANES)) == 8 * g + row_of((8, LANES))
    placed = jnp.sum(jnp.where(mine, jnp.broadcast_to(partial, (8, LANES)), 0.0), axis=0, keepdims=True)

    def sum_over(value, landing, offsets, peer, index):
        landing[0] = value
        for slot, offset in enumerate(offsets, 1):
            remote(
                landing.at[0], landing.at[slot], many_send.at[index], many_recv.at[index], peer(*offset)
            ).start()
        wait_bytes(landing.at[pl.ds(1, len(offsets))], many_recv.at[index])
        return jnp.sum(landing[...], axis=0)

    plane_sum = sum_over(placed, part_in, plane_offsets, plane_peer, 3)
    coef_out[...] = sum_over(plane_sum, sum_in, line_offsets, line_peer, 4)

    for copy in copies + velocity_rims + copies2:
        copy.wait_send()
    wait_bytes(slots_in.at[pl.ds(0, n_tile - 1)], many_send.at[0])
    wait_bytes(early_in.at[pl.ds(0, len(direct))], many_send.at[1])
    wait_bytes(early_in.at[0], hand_send.at[0])
    if handed_on:
        wait_bytes(early_in.at[pl.ds(0, len(handed_on))], hand_send.at[1])
    wait_bytes(late_in.at[pl.ds(0, n_grp - 1)], many_send.at[2])
    wait_bytes(part_in.at[pl.ds(1, len(plane_offsets))], many_send.at[3])
    wait_bytes(sum_in.at[pl.ds(1, len(line_offsets))], many_send.at[4])


def hand_out(a, b, c, a_out, b_out, c_out, sems):
    copies = [
        pltpu.make_async_copy(src, dst, sems.at[index])
        for index, (src, dst) in enumerate(((a, a_out), (b, b_out), (c, c_out)))
    ]
    for copy in copies:
        copy.start()
    for copy in copies:
        copy.wait()


def on_device(n_grp, n_tile, base_velocity, viscosity, friction, friction_probe, pixel_los, pixel_weight, pixel_cell, pixel_count, panels):
    slots = pixel_los.shape[-1]
    panel_rows = panels.shape[1]
    vmem = pl.BlockSpec(memory_space=pltpu.VMEM)
    hbm = pl.BlockSpec(memory_space=pltpu.HBM)
    wide = 64 + 2 * HALO
    increment, probe, coefficients = pl.pallas_call(
        functools.partial(kernel, n_grp, n_tile),
        out_shape=(
            pltpu.VMEM((2, 64, LANES), F32),
            pltpu.VMEM((64, LANES), F32),
            pltpu.VMEM((1, LANES), F32),
        ),
        in_specs=[hbm] * 9,
        out_specs=(vmem, vmem, vmem),
        scratch_shapes=[
            pltpu.VMEM((2, wide, LANES), F32),
            pltpu.VMEM((64, LANES), F32),
            pltpu.VMEM((64, LANES), F32),
            pltpu.VMEM((64, LANES), F32),
            pltpu.VMEM((2, slots), F32),
            pltpu.VMEM((1, slots), F32),
            pltpu.VMEM((1, slots), jnp.int32),
            pltpu.SMEM((1, n_tile), jnp.int32),
            pltpu.VMEM((4, wide, LANES), F32),
            pltpu.VMEM((48, LANES), F32),
            pltpu.VMEM((48, LANES), F32),
            pltpu.VMEM((48, LANES), F32),
            pltpu.VMEM((n_tile // 2, 4, LANES), F32),
            pltpu.VMEM((n_tile, 4, LANES), F32),
            pltpu.VMEM((10, 2, wide, LANES), F32),
            pltpu.VMEM((2, 2, wide, LANES), F32),
            pltpu.VMEM((2, 2, wide + 2 * HALO, LANES), F32),
            pltpu.VMEM((2, 2, wide + 2 * HALO, LANES), F32),
            pltpu.VMEM((2, wide, LANES), F32),
            pltpu.VMEM((32, LANES), F32),
            pltpu.VMEM((32, LANES), F32),
            pltpu.VMEM((32, LANES), F32),
            pltpu.VMEM((wide, LANES), BF16),
            pltpu.VMEM((n_grp, wide, LANES), BF16),
            pltpu.VMEM((16, LANES), BF16),
            pltpu.VMEM((n_grp, 16, LANES), BF16),
            pltpu.VMEM((panel_rows + 2 * HALO, LANES), F32),
            pltpu.VMEM((8, panel_rows, LANES), BF16),
            pltpu.VMEM((panel_rows + 2 * HALO, LANES), F32),
            pltpu.VMEM((8, n_grp, 16, LANES), F32),
            pltpu.VMEM((2 * n_grp, 1, LANES), F32),
            pltpu.VMEM((n_tile // 2, 1, LANES), F32),
            pltpu.SemaphoreType.DMA((8,)),
            pltpu.SemaphoreType.DMA((8,)),
            pltpu.SemaphoreType.DMA((8,)),
            pltpu.SemaphoreType.DMA((8,)),
            pltpu.SemaphoreType.DMA((2,)),
            pltpu.SemaphoreType.DMA((2,)),
            pltpu.SemaphoreType.DMA((2,)),
            pltpu.SemaphoreType.DMA((2,)),
            pltpu.SemaphoreType.DMA((9,)),
            pltpu.SemaphoreType.DMA((5,)),
            pltpu.SemaphoreType.DMA((5,)),
        ],
        compiler_params=pltpu.CompilerParams(
            collective_id=0, has_side_effects=True, vmem_limit_bytes=24 * 1024 * 1024
        ),
    )(
        *(
            pltpu.with_memory_space_constraint(a, pltpu.HBM)
            for a in (
                base_velocity,
                viscosity,
                friction,
                friction_probe,
                pixel_los,
                pixel_weight,
                pixel_cell,
                pixel_count,
                panels,
            )
        )
    )
    increment, probe, coefficients = pl.pallas_call(
        hand_out,
        out_shape=(
            jax.ShapeDtypeStruct((2, 64, LANES), F32),
            jax.ShapeDtypeStruct((64, LANES), F32),
            jax.ShapeDtypeStruct((1, LANES), F32),
        ),
        in_specs=[vmem] * 3,
        out_specs=(hbm, hbm, hbm),
        scratch_shapes=[pltpu.SemaphoreType.DMA((3,))],
    )(*(pltpu.with_memory_space_constraint(a, pltpu.VMEM) for a in (increment, probe, coefficients)))
    return increment, probe, coefficients.reshape(LANES)[: 8 * n_grp]


def solution(mesh):
    in_specs = (
        P(None, "grp", "tile"),
        P("grp", "tile"),
        P("grp", "tile"),
        P("grp", "tile"),
        P("grp", "tile", None, None),
        P("grp", "tile", None, None),
        P("grp", "tile", None, None),
        P("grp", "tile", None, None),
        P("grp", None, "tile"),
    )
    out_specs = (P(None, "grp", "tile"), P("grp", "tile"), P())
    body = functools.partial(on_device, mesh.shape["grp"], mesh.shape["tile"])
    return jax.shard_map(body, mesh=mesh, in_specs=in_specs, out_specs=out_specs, check_vma=False)
```

```python
import functools

import jax
import jax.numpy as jnp
from jax import lax
from jax.experimental import pallas as pl
from jax.experimental.pallas import tpu as pltpu
from jax.sharding import PartitionSpec as P

SWEEPS = 8
RELAX = 0.8
HALO = 8
CAP = 64
LANES = 128
MESH = pl.DeviceIdType.MESH
F32 = jnp.float32
BF16 = jnp.bfloat16


def lane_of(shape):
    return lax.broadcasted_iota(jnp.int32, shape, 1)


def row_of(shape):
    return lax.broadcasted_iota(jnp.int32, shape, 0)


def row_next(a):
    return pltpu.roll(a, a.shape[0] - 1, 0)


def row_prev(a):
    return pltpu.roll(a, 1, 0)


def col_next(a):
    return pltpu.roll(a, a.shape[1] - 1, 1)


def col_prev(a):
    return pltpu.roll(a, 1, 1)


def pack_rims(fields):
    lane = lane_of(fields[0].shape)
    packed = pltpu.roll(fields[0], 8, 1)
    for index, field in enumerate(fields[1:], 1):
        moved = pltpu.roll(field, 16 * index + 8, 1)
        packed = jnp.where(lane >= 16 * index, moved, packed)
    return packed


def fold_rows(packed, width):
    high = width // 2
    folded = packed[0:high]
    lane = lane_of(folded.shape)
    for index in range(1, LANES // width):
        moved = pltpu.roll(packed[index * high : (index + 1) * high], index * width, 1)
        folded = jnp.where(lane >= index * width, moved, folded)
    return folded


def unfold_rows(folded, width):
    parts = [folded] + [pltpu.roll(folded, LANES - index * width, 1) for index in range(1, LANES // width)]
    return jnp.concatenate(parts, axis=0)


def ring(offset, size):
    return min(offset % size, -offset % size)


def far_first(pairs, distance):
    return sorted((p for p in pairs if any(p)), key=lambda p: (-distance(*p), p))


def kernel(
    n_grp,
    n_tile,
    base_velocity_in,
    viscosity_in,
    friction_in,
    friction_probe_in,
    pixel_los_in,
    pixel_weight_in,
    pixel_cell_in,
    pixel_count_in,
    panels,
    increment_out,
    probe_out,
    coef_out,
    base_velocity,
    viscosity,
    friction,
    friction_probe,
    pixel_los,
    pixel_weight,
    pixel_cell,
    pixel_count,
    ext,
    pack,
    side_r,
    side_l,
    slots_out,
    slots_in,
    coef,
    src,
    field,
    other,
    strip_coef,
    strip_src,
    strip,
    strip_other,
    ext2,
    pack2,
    side2_r,
    side2_l,
    early_stage,
    early_in,
    late_stage,
    late_in,
    column,
    panel_buf,
    panel_ext,
    panel_rim,
    part_in,
    sum_in,
    halo_send,
    halo_recv,
    halo2_send,
    halo2_recv,
    rim_send,
    rim_recv,
    hand_send,
    hand_recv,
    local_sem,
    many_send,
    many_recv,
):
    g = lax.axis_index("grp")
    t = lax.axis_index("tile")
    up = lax.rem(g + n_grp - 1, n_grp)
    down = lax.rem(g + 1, n_grp)
    left = lax.rem(t + n_tile - 1, n_tile)
    right = lax.rem(t + 1, n_tile)

    y_size = 4
    x_size = n_grp // y_size
    z_size = n_tile // 4
    x, y_hi = lax.div(g, y_size), lax.rem(g, y_size)
    z, y_lo, core = lax.div(t, 4), lax.rem(lax.div(t, 2), 2), lax.rem(t, 2)
    y = 2 * y_hi + y_lo

    def tile_peer(dz, flip):
        lo = 1 - y_lo if flip >= 2 else y_lo
        side = 1 - core if flip % 2 else core
        return (g, 4 * lax.rem(z + dz, z_size) + 2 * lo + side)

    def grp_peer(dx, dy):
        return (y_size * lax.rem(x + dx, x_size) + lax.rem(y_hi + dy, y_size), t)

    def plane_peer(dx, dy):
        there = lax.rem(y + dy, 2 * y_size)
        return (y_size * lax.rem(x + dx, x_size) + lax.div(there, 2), 4 * z + 2 * lax.rem(there, 2) + core)

    def line_peer(dz, flip):
        return (g, 4 * lax.rem(z + dz, z_size) + 2 * y_lo + (1 - core if flip else core))

    tile_offsets = far_first(
        [(dz, flip) for dz in range(z_size) for flip in range(4)], lambda dz, flip: ring(dz, z_size) + (flip >= 2)
    )
    grp_offsets = far_first(
        [(dx, dy) for dx in range(x_size) for dy in range(y_size)],
        lambda dx, dy: ring(dx, x_size) + 2 * ring(dy, y_size),
    )
    plane_offsets = far_first(
        [(dx, dy) for dx in range(x_size) for dy in range(2 * y_size)],
        lambda dx, dy: ring(dx, x_size) + ring(dy, 2 * y_size),
    )
    line_offsets = far_first(
        [(dz, flip) for dz in range(z_size) for flip in range(2)], lambda dz, flip: ring(dz, z_size)
    )

    barrier = pltpu.get_barrier_semaphore()
    corners = [(a, b) for a in (up, down) for b in (left, right)]
    across = [plane_peer(*p) for p in plane_offsets if p[1] % 2]
    peers = corners + [(up, t), (down, t), (g, left), (g, right)]
    peers += [grp_peer(*p) for p in grp_offsets] + across + [tile_peer(*p) for p in tile_offsets if p != (0, 2)]
    for peer in peers:
        pl.semaphore_signal(barrier, inc=1, device_id=peer, device_id_type=MESH)

    loads = [
        pltpu.make_async_copy(a, b, local_sem.at[1 + index])
        for index, (a, b) in enumerate(
            [
                (base_velocity_in, base_velocity.at[:, pl.ds(HALO, 64)]),
                (viscosity_in, viscosity),
                (friction_in, friction),
                (friction_probe_in, friction_probe),
                (pixel_los_in.at[0, 0], pixel_los),
                (pixel_weight_in.at[0, 0], pixel_weight),
                (pixel_cell_in.at[0, 0], pixel_cell),
                (pixel_count_in.at[0, 0], pixel_count),
            ]
        )
    ]
    for load in loads:
        load.start()

    panel_copy = pltpu.make_async_copy(panels, panel_buf, local_sem.at[0])
    panel_copy.start()

    for load in loads[:4]:
        load.wait()
    bvx = base_velocity[0, HALO : HALO + 64]
    bvy = base_velocity[1, HALO : HALO + 64]
    fp = friction_probe[...]
    own = (viscosity[...], friction[...], -(fp * bvx), -(fp * bvy))
    for index in range(4):
        ext[index, HALO : HALO + 64, :] = own[index]
    packed = pack_rims(own)
    pack[0:8] = packed[0:8]
    pack[8:40] = fold_rows(packed, 64)
    pack[40:48] = packed[56:64]

    for load in loads[4:]:
        load.wait()
    odd = lax.rem(t, 2)
    lane1 = lane_of((1, LANES))
    for pair in range(n_tile // 2):
        lanes = slice(pair * LANES, (pair + 1) * LANES)
        count = jnp.where(lane1 < CAP, pixel_count[0, 2 * pair], pixel_count[0, 2 * pair + 1])
        live = lax.rem(lane1, CAP) < count
        block = jnp.concatenate(
            [
                pixel_los[:, lanes],
                jnp.where(live, pixel_weight[:, lanes], 0.0),
                pixel_cell[:, lanes].astype(F32),
            ],
            axis=0,
        )
        slots_out[pair] = jnp.where(odd == 1, pltpu.roll(block, CAP, 1), block)

    pl.semaphore_wait(barrier, len(peers))

    def remote(src_ref, dst_ref, send_sem, recv_sem, peer):
        return pltpu.make_async_remote_copy(
            src_ref=src_ref,
            dst_ref=dst_ref,
            send_sem=send_sem,
            recv_sem=recv_sem,
            device_id=peer,
            device_id_type=MESH,
        )

    def rim_copies(block, packed, from_right, from_left, send, recv):
        first, last = pl.ds(HALO, HALO), pl.ds(64, HALO)
        above, below = pl.ds(0, HALO), pl.ds(64 + HALO, HALO)
        high = packed.shape[0] - 16
        head, middle, tail = pl.ds(0, 8), pl.ds(8, high), pl.ds(8 + high, 8)
        moves = [
            (packed.at[head], from_right.at[tail], (up, left)),
            (packed.at[head], from_left.at[tail], (up, right)),
            (packed.at[tail], from_right.at[head], (down, left)),
            (packed.at[tail], from_left.at[head], (down, right)),
            (block.at[:, first], block.at[:, below], (up, t)),
            (block.at[:, last], block.at[:, above], (down, t)),
            (packed.at[middle], from_right.at[middle], (g, left)),
            (packed.at[middle], from_left.at[middle], (g, right)),
        ]
        return [remote(a, b, send.at[index], recv.at[index], peer) for index, (a, b, peer) in enumerate(moves)]

    def wait_bytes(ref, sem):
        pltpu.make_async_copy(ref, ref, sem).wait()

    copies = rim_copies(ext, pack, side_r, side_l, halo_send, halo_recv)
    for copy in copies:
        copy.start()
    first, last = pl.ds(HALO, HALO), pl.ds(64, HALO)
    above, below = pl.ds(0, HALO), pl.ds(64 + HALO, HALO)
    velocity_rims = [
        remote(base_velocity.at[:, first], base_velocity.at[:, below], rim_send.at[0], rim_recv.at[0], (up, t)),
        remote(base_velocity.at[:, last], base_velocity.at[:, above], rim_send.at[1], rim_recv.at[1], (down, t)),
    ]
    for copy in velocity_rims:
        copy.start()

    for dz, flip in tile_offsets:
        peer = tile_peer(dz, flip)
        remote(
            slots_out.at[lax.div(peer[1], 2)], slots_in.at[4 * dz + flip], many_send.at[0], many_recv.at[0], peer
        ).start()
    slots_in[0] = slots_out[lax.div(t, 2)]

    for copy in copies:
        copy.wait_recv()

    rows = 64 + 2 * HALO
    lane = lane_of((rows, LANES))
    row = row_of((rows, LANES))

    def merge(from_right, from_left):
        return jnp.where(lax.rem(lane_of(from_right.shape), 16) >= 8, from_right, from_left)

    def beside(merged, index):
        return pltpu.roll(merged, LANES - 16 * index - 8, 1)

    def widen(block, from_right, from_left):
        merged = merge(from_right[...], from_left[...])
        high = merged.shape[0] - 16
        middle = unfold_rows(merged[8 : 8 + high], 2 * high)
        merged = jnp.concatenate([merged[0:8], middle, merged[8 + high :]], axis=0)
        return [
            jnp.concatenate([block[index], beside(merged, index)], axis=1) for index in range(block.shape[0])
        ]

    v, fr, sx, sy = widen(ext, side_r, side_l)
    row_inside = ((row >= HALO) | (g > 0)) & ((row < HALO + 64) | (g < n_grp - 1))
    col_inside = ((lane < HALO) & (t < n_tile - 1)) | ((lane >= LANES - HALO) & (t > 0))
    inside = jnp.concatenate([row_inside, row_inside & col_inside], axis=1)
    v = jnp.where(inside, v, 0.0)
    pair_sum = v + row_next(v)
    east = 0.5 * pair_sum
    west = row_prev(east)
    north = 0.5 * (v + col_next(v))
    south = col_prev(north)
    node_pp = 0.0625 * (pair_sum + col_next(pair_sum))
    node_mp = row_prev(node_pp)
    node_pm = col_prev(node_pp)
    node_mm = col_prev(node_mp)
    diag_x = fr + 2.0 * (east + west) + (north + south)
    diag_y = fr + (east + west) + 2.0 * (north + south)
    inv_x = jnp.where(inside, RELAX / jnp.where(inside, diag_x, 1.0), 0.0)
    inv_y = jnp.where(inside, RELAX / jnp.where(inside, diag_y, 1.0), 0.0)
    for index, term in enumerate((east, west, north, south, node_pp, node_mp, node_pm, node_mm, inv_x, inv_y)):
        coef[index, 0] = term[:, :LANES]
        coef[index, 1] = term[:, LANES:]
    for index, term in enumerate((sx, sy)):
        src[index, 0] = term[:, :LANES]
        src[index, 1] = term[:, LANES:]
    for buffer in (field, other):
        buffer[:, :, 0:HALO] = jnp.zeros((2, 2, HALO, LANES), F32)
        buffer[:, :, HALO + rows :] = jnp.zeros((2, 2, HALO, LANES), F32)
    tile_lane = lane_of((8, LANES))
    at_last, at_first = tile_lane == LANES - 1, tile_lane == 0

    def pair_next(pair):
        own, rim = (pltpu.roll(a, LANES - 1, 1) for a in pair)
        return jnp.where(at_last, rim, own), jnp.where(at_last, own, rim)

    def pair_prev(pair):
        own, rim = (pltpu.roll(a, 1, 1) for a in pair)
        return jnp.where(at_first, rim, own), jnp.where(at_first, own, rim)

    def sweep(now, later):
        for tile in range(rows // 8):
            at = slice(8 * tile, 8 * tile + 8)
            inner = slice(8 * tile + HALO, 8 * tile + HALO + 8)
            after = slice(8 * tile + HALO + 1, 8 * tile + HALO + 9)
            before = slice(8 * tile + HALO - 1, 8 * tile + HALO + 7)
            axial, forward, backward, centre = ([], []), ([], []), ([], []), ([], [])
            for part in range(2):
                e, w, n, s, pp, mp, pm, mm = (coef[index, part, at] for index in range(8))
                cx, cy = now[0, part, inner], now[1, part, inner]
                ux, uy = now[0, part, after], now[1, part, after]
                dx, dy = now[0, part, before], now[1, part, before]
                ax = e * ux + w * dx
                cy2 = cy + cy
                axial[0].append(ax + ax)
                axial[1].append(e * uy + w * dy)
                forward[0].append(s * cx + (pm * uy - mm * dy))
                forward[1].append(s * cy2 + (pm * ux - mm * dx))
                backward[0].append(n * cx + (mp * dy - pp * uy))
                backward[1].append(n * cy2 + (mp * dx - pp * ux))
                centre[0].append(cx)
                centre[1].append(cy)
            for index in range(2):
                ahead, behind = pair_next(forward[index]), pair_prev(backward[index])
                for part in range(2):
                    total = src[index, part, at] + axial[index][part] + (ahead[part] + behind[part])
                    later[index, part, inner] = (1.0 - RELAX) * centre[index][part] + (
                        coef[8 + index, part, at] * total
                    )

    def two_sweeps(_, carry):
        sweep(other, field)
        sweep(field, other)
        return carry

    def relax():
        for index in range(2):
            other[index, :, HALO : HALO + rows] = coef[8 + index] * src[index]
        lax.fori_loop(0, (SWEEPS - 2) // 2, two_sweeps, 0)
        sweep(other, field)

    def solved(index, at):
        return field[index, 0, at.start + HALO : at.stop + HALO]

    def probe_of(at):
        return -(base_velocity[0, at] * solved(0, at) + base_velocity[1, at] * solved(1, at))

    own_rows = slice(HALO, HALO + 64)
    relax()
    inc_x, inc_y = solved(0, own_rows), solved(1, own_rows)
    increment_out[0] = inc_x
    increment_out[1] = inc_y

    wait_bytes(slots_in.at[pl.ds(0, n_tile - 1)], many_recv.at[0])

    def halves(a):
        high = a.astype(BF16)
        return high, (a - high.astype(F32)).astype(BF16)

    xh, xl = halves(inc_x)
    yh, yl = halves(inc_y)
    stacked = jnp.concatenate([xh, yh, xl, yl], axis=0)
    chunk = 2 * LANES
    total = jnp.zeros((256, LANES), F32)
    low_half = lane_of((4, LANES)) < CAP
    for index in range(n_tile * CAP // chunk):
        first = jnp.where(low_half, slots_in[4 * index], slots_in[4 * index + 1])
        second = jnp.where(low_half, slots_in[4 * index + 2], slots_in[4 * index + 3])
        lists = jnp.concatenate([first, second], axis=1)
        los_x, los_y, weight = lists[0:1], lists[1:2], lists[2:3]
        cell = lists[3:4].astype(jnp.int32)
        at_col = row_of((LANES, chunk)) == (cell & (LANES - 1))
        at_row = row_of((64, chunk)) == (cell >> 7)
        col_hot = jnp.where(at_col, 1.0, 0.0).astype(BF16)
        found = jnp.dot(stacked, col_hot, preferred_element_type=F32)
        got_x = jnp.sum(jnp.where(at_row, found[0:64] + found[128:192], 0.0), axis=0, keepdims=True)
        got_y = jnp.sum(jnp.where(at_row, found[64:128] + found[192:256], 0.0), axis=0, keepdims=True)
        amount = weight * (los_x * got_x + los_y * got_y)
        scaled = []
        for value in (amount * los_x, amount * los_y):
            high = value.astype(BF16).astype(F32)
            scaled.append((high, value - high))
        hot = [
            jnp.where(at_row, jnp.broadcast_to(part, (64, chunk)), 0.0)
            for part in (scaled[0][0], scaled[1][0], scaled[0][1], scaled[1][1])
        ]
        hot = jnp.concatenate(hot, axis=0).astype(BF16)
        total += lax.dot_general(hot, col_hot, (((1,), (1,)), ((), ())), preferred_element_type=F32)
    adjoint = (total[0:64] + total[128:192], total[64:128] + total[192:256])

    for index in range(2):
        ext2[index, HALO : HALO + 64, :] = adjoint[index]
    packed2 = pack_rims(adjoint)
    pack2[0:8] = packed2[0:8]
    pack2[8:24] = fold_rows(packed2, 32)
    pack2[24:32] = packed2[56:64]
    copies2 = rim_copies(ext2, pack2, side2_r, side2_l, halo2_send, halo2_recv)
    for copy in copies2[6:] + copies2[:6]:
        copy.start()

    for index in range(2):
        src[index] = jnp.zeros((2, rows, LANES), F32)
        src[index, 0, own_rows] = adjoint[index]
    relax()
    for copy in velocity_rims:
        copy.wait_recv()
    everything = slice(0, rows)
    part = probe_of(everything).astype(BF16)
    early_stage[...] = part
    early_in[g] = part
    opposite = grp_peer(0, y_size // 2)
    handed_on = [(dx, 0) for dx in range(1, x_size)]
    direct = [offset for offset in grp_offsets if offset[1] != y_size // 2]
    remote(early_stage, early_in.at[g], hand_send.at[0], hand_recv.at[0], opposite).start()
    for offset in direct:
        remote(early_stage, early_in.at[g], many_send.at[1], many_recv.at[1], grp_peer(*offset)).start()

    panel_copy.wait()
    panel_ext[0:HALO] = jnp.zeros((HALO, LANES), F32)
    panel_ext[HALO + 64 * n_grp :] = jnp.zeros((HALO, LANES), F32)
    fold_lane = lane_of((16, LANES))

    def fold_late(block, start):
        folded = jnp.zeros((16, LANES), F32)
        for j in range(rows // 16):
            moved = pltpu.roll(block[start + 16 * j : start + 16 * j + 16, :], 16 * j + 8, 1)
            here = (fold_lane >= 16 * j) & (fold_lane < 16 * j + 16)
            folded = jnp.where(here, moved, folded)
        return folded

    def fold_panel(k, carry):
        panel_ext[HALO : HALO + 64 * n_grp] = panel_buf[k].astype(F32)
        for block in range(n_grp):
            panel_rim[k, block] = fold_late(panel_ext, 64 * block)
        return carry

    lax.fori_loop(0, 8, fold_panel, 0)

    near_left = (lane < 8) | (lane >= 120)
    near_right = (lane >= 56) & (lane < 72)
    for index in range(10):
        left_strip = jnp.where(lane < 64, coef[index, 0], coef[index, 1])
        right_strip = pltpu.roll(jnp.where(lane < 64, coef[index, 1], coef[index, 0]), 64, 1)
        strip_coef[index] = jnp.where(near_left, left_strip, jnp.where(near_right, right_strip, 0.0))
    strip_src[...] = jnp.zeros((2, rows, LANES), F32)
    for buffer in (strip, strip_other):
        buffer[...] = jnp.zeros((2, rows + 2 * HALO, LANES), F32)

    def strip_sweep(now, later):
        for tile in range(rows // 8):
            at = slice(8 * tile, 8 * tile + 8)
            inner = slice(8 * tile + HALO, 8 * tile + HALO + 8)
            after = slice(8 * tile + HALO + 1, 8 * tile + HALO + 9)
            before = slice(8 * tile + HALO - 1, 8 * tile + HALO + 7)
            e, w, n, s, pp, mp, pm, mm = (strip_coef[index, at] for index in range(8))
            cx, cy = now[0, inner], now[1, inner]
            ux, uy = now[0, after], now[1, after]
            dx, dy = now[0, before], now[1, before]
            ax = e * ux + w * dx
            cy2 = cy + cy
            ax = ax + ax + (col_next(s * cx + (pm * uy - mm * dy)) + col_prev(n * cx + (mp * dy - pp * uy)))
            ay = e * uy + w * dy
            ay = ay + (col_next(s * cy2 + (pm * ux - mm * dx)) + col_prev(n * cy2 + (mp * dx - pp * ux)))
            later[0, inner] = (1.0 - RELAX) * cx + strip_coef[8, at] * (strip_src[0, at] + ax)
            later[1, inner] = (1.0 - RELAX) * cy + strip_coef[9, at] * (strip_src[1, at] + ay)

    def two_strip_sweeps(_, carry):
        strip_sweep(strip_other, strip)
        strip_sweep(strip, strip_other)
        return carry

    for copy in copies2[6:]:
        copy.wait_recv()
    middle = unfold_rows(merge(side2_r[8:24], side2_l[8:24]), 32)
    rim_lane = lane_of((64, LANES))
    for index in range(2):
        rim = beside(middle, index)
        src[index, 1, own_rows] = rim
        moved = jnp.where((rim_lane >= 64) & (rim_lane < 72), pltpu.roll(rim, 64, 1), 0.0)
        strip_src[index, own_rows] = jnp.where(rim_lane >= 120, rim, moved)
    for index in range(2):
        strip_other[index, HALO : HALO + rows] = strip_coef[8 + index] * strip_src[index]
    lax.fori_loop(0, (SWEEPS - 2) // 2, two_strip_sweeps, 0)
    strip_sweep(strip_other, strip)
    total = []
    for index in range(2):
        added = strip[index, HALO : HALO + rows]
        added = jnp.where(lane < 64, added, pltpu.roll(added, 64, 1))
        total.append(solved(index, everything) + added)
    late = -(base_velocity[0] * total[0] + base_velocity[1] * total[1])
    late = fold_late(late, 0).astype(BF16)
    late_stage[...] = late
    late_in[g] = late
    for offset in grp_offsets:
        remote(late_stage, late_in.at[g], many_send.at[2], many_recv.at[2], grp_peer(*offset)).start()

    wait_bytes(early_in.at[0], hand_recv.at[0])
    for offset in handed_on:
        remote(
            early_in.at[opposite[0]], early_in.at[opposite[0]], hand_send.at[1], hand_recv.at[1], grp_peer(*offset)
        ).start()

    for copy in copies2[:6]:
        copy.wait_recv()
    for at, edge in ((slice(0, 8), slice(0, 8)), (slice(64 + HALO, rows), slice(24, 32))):
        merged = merge(side2_r[edge], side2_l[edge])
        for index in range(2):
            src[index, 0, at] = ext2[index, at]
            src[index, 1, at] = beside(merged, index)
    relax()
    probe_out[...] = probe_of(own_rows)

    wait_bytes(early_in.at[pl.ds(0, len(direct))], many_recv.at[1])
    if handed_on:
        wait_bytes(early_in.at[pl.ds(0, len(handed_on))], hand_recv.at[1])
    column[...] = jnp.zeros_like(column)
    part_lane = lane_of((rows, LANES))
    is_middle = (part_lane >= HALO) & (part_lane < LANES - HALO)
    for block in range(n_grp):
        at = slice(64 * block, 64 * block + rows)
        column[at] += jnp.where(is_middle, early_in[block].astype(F32), 0.0)

    def project(block, sums):
        start = pl.multiple_of(block * 64, 64)
        values = column[pl.ds(start + HALO, 64), :]
        return tuple(
            total + jnp.sum((panel_buf[k, pl.ds(start, 64), :].astype(F32) * values).reshape(8, 8, LANES), axis=0)
            for k, total in enumerate(sums)
        )

    sums = lax.fori_loop(0, n_grp, project, tuple(jnp.zeros((8, LANES), F32) for _ in range(8)))
    wait_bytes(late_in.at[pl.ds(0, n_grp - 1)], many_recv.at[2])
    sums = list(sums)
    for block in range(n_grp):
        late = late_in[block].astype(F32)
        for k in range(8):
            product = panel_rim[k, block] * late
            sums[k] = sums[k] + product[0:8] + product[8:16]
    partial = jnp.concatenate([jnp.sum(s, axis=0, keepdims=True) for s in sums], axis=0)
    partial = jnp.sum(partial, axis=1, keepdims=True)
    mine = lane_of((8, LANES)) == 8 * g + row_of((8, LANES))
    placed = jnp.sum(jnp.where(mine, jnp.broadcast_to(partial, (8, LANES)), 0.0), axis=0, keepdims=True)

    def sum_over(value, landing, offsets, peer, index):
        landing[0] = value
        for slot, offset in enumerate(offsets, 1):
            remote(
                landing.at[0], landing.at[slot], many_send.at[index], many_recv.at[index], peer(*offset)
            ).start()
        wait_bytes(landing.at[pl.ds(1, len(offsets))], many_recv.at[index])
        return jnp.sum(landing[...], axis=0)

    plane_sum = sum_over(placed, part_in, plane_offsets, plane_peer, 3)
    coef_out[...] = sum_over(plane_sum, sum_in, line_offsets, line_peer, 4)

    for copy in copies + velocity_rims + copies2:
        copy.wait_send()
    wait_bytes(slots_in.at[pl.ds(0, n_tile - 1)], many_send.at[0])
    wait_bytes(early_in.at[pl.ds(0, len(direct))], many_send.at[1])
    wait_bytes(early_in.at[0], hand_send.at[0])
    if handed_on:
        wait_bytes(early_in.at[pl.ds(0, len(handed_on))], hand_send.at[1])
    wait_bytes(late_in.at[pl.ds(0, n_grp - 1)], many_send.at[2])
    wait_bytes(part_in.at[pl.ds(1, len(plane_offsets))], many_send.at[3])
    wait_bytes(sum_in.at[pl.ds(1, len(line_offsets))], many_send.at[4])


def hand_out(a, b, c, a_out, b_out, c_out, sems):
    copies = [
        pltpu.make_async_copy(src, dst, sems.at[index])
        for index, (src, dst) in enumerate(((a, a_out), (b, b_out), (c, c_out)))
    ]
    for copy in copies:
        copy.start()
    for copy in copies:
        copy.wait()


def on_device(n_grp, n_tile, base_velocity, viscosity, friction, friction_probe, pixel_los, pixel_weight, pixel_cell, pixel_count, panels):
    slots = pixel_los.shape[-1]
    panel_rows = panels.shape[1]
    vmem = pl.BlockSpec(memory_space=pltpu.VMEM)
    hbm = pl.BlockSpec(memory_space=pltpu.HBM)
    wide = 64 + 2 * HALO
    increment, probe, coefficients = pl.pallas_call(
        functools.partial(kernel, n_grp, n_tile),
        out_shape=(
            pltpu.VMEM((2, 64, LANES), F32),
            pltpu.VMEM((64, LANES), F32),
            pltpu.VMEM((1, LANES), F32),
        ),
        in_specs=[hbm] * 9,
        out_specs=(vmem, vmem, vmem),
        scratch_shapes=[
            pltpu.VMEM((2, wide, LANES), F32),
            pltpu.VMEM((64, LANES), F32),
            pltpu.VMEM((64, LANES), F32),
            pltpu.VMEM((64, LANES), F32),
            pltpu.VMEM((2, slots), F32),
            pltpu.VMEM((1, slots), F32),
            pltpu.VMEM((1, slots), jnp.int32),
            pltpu.SMEM((1, n_tile), jnp.int32),
            pltpu.VMEM((4, wide, LANES), F32),
            pltpu.VMEM((48, LANES), F32),
            pltpu.VMEM((48, LANES), F32),
            pltpu.VMEM((48, LANES), F32),
            pltpu.VMEM((n_tile // 2, 4, LANES), F32),
            pltpu.VMEM((n_tile, 4, LANES), F32),
            pltpu.VMEM((10, 2, wide, LANES), F32),
            pltpu.VMEM((2, 2, wide, LANES), F32),
            pltpu.VMEM((2, 2, wide + 2 * HALO, LANES), F32),
            pltpu.VMEM((2, 2, wide + 2 * HALO, LANES), F32),
            pltpu.VMEM((10, wide, LANES), F32),
            pltpu.VMEM((2, wide, LANES), F32),
            pltpu.VMEM((2, wide + 2 * HALO, LANES), F32),
            pltpu.VMEM((2, wide + 2 * HALO, LANES), F32),
            pltpu.VMEM((2, wide, LANES), F32),
            pltpu.VMEM((32, LANES), F32),
            pltpu.VMEM((32, LANES), F32),
            pltpu.VMEM((32, LANES), F32),
            pltpu.VMEM((wide, LANES), BF16),
            pltpu.VMEM((n_grp, wide, LANES), BF16),
            pltpu.VMEM((16, LANES), BF16),
            pltpu.VMEM((n_grp, 16, LANES), BF16),
            pltpu.VMEM((panel_rows + 2 * HALO, LANES), F32),
            pltpu.VMEM((8, panel_rows, LANES), BF16),
            pltpu.VMEM((panel_rows + 2 * HALO, LANES), F32),
            pltpu.VMEM((8, n_grp, 16, LANES), F32),
            pltpu.VMEM((2 * n_grp, 1, LANES), F32),
            pltpu.VMEM((n_tile // 2, 1, LANES), F32),
            pltpu.SemaphoreType.DMA((8,)),
            pltpu.SemaphoreType.DMA((8,)),
            pltpu.SemaphoreType.DMA((8,)),
            pltpu.SemaphoreType.DMA((8,)),
            pltpu.SemaphoreType.DMA((2,)),
            pltpu.SemaphoreType.DMA((2,)),
            pltpu.SemaphoreType.DMA((2,)),
            pltpu.SemaphoreType.DMA((2,)),
            pltpu.SemaphoreType.DMA((9,)),
            pltpu.SemaphoreType.DMA((5,)),
            pltpu.SemaphoreType.DMA((5,)),
        ],
        compiler_params=pltpu.CompilerParams(
            collective_id=0, has_side_effects=True, vmem_limit_bytes=24 * 1024 * 1024
        ),
    )(
        *(
            pltpu.with_memory_space_constraint(a, pltpu.HBM)
            for a in (
                base_velocity,
                viscosity,
                friction,
                friction_probe,
                pixel_los,
                pixel_weight,
                pixel_cell,
                pixel_count,
                panels,
            )
        )
    )
    increment, probe, coefficients = pl.pallas_call(
        hand_out,
        out_shape=(
            jax.ShapeDtypeStruct((2, 64, LANES), F32),
            jax.ShapeDtypeStruct((64, LANES), F32),
            jax.ShapeDtypeStruct((1, LANES), F32),
        ),
        in_specs=[vmem] * 3,
        out_specs=(hbm, hbm, hbm),
        scratch_shapes=[pltpu.SemaphoreType.DMA((3,))],
    )(*(pltpu.with_memory_space_constraint(a, pltpu.VMEM) for a in (increment, probe, coefficients)))
    return increment, probe, coefficients.reshape(LANES)[: 8 * n_grp]


def solution(mesh):
    in_specs = (
        P(None, "grp", "tile"),
        P("grp", "tile"),
        P("grp", "tile"),
        P("grp", "tile"),
        P("grp", "tile", None, None),
        P("grp", "tile", None, None),
        P("grp", "tile", None, None),
        P("grp", "tile", None, None),
        P("grp", None, "tile"),
    )
    out_specs = (P(None, "grp", "tile"), P("grp", "tile"), P())
    body = functools.partial(on_device, mesh.shape["grp"], mesh.shape["tile"])
    return jax.shard_map(body, mesh=mesh, in_specs=in_specs, out_specs=out_specs, check_vma=False)
```
